32 devices in a mesh: groups: 2 (over x), tile: 16 (over z, y, core).
Axes of the slice: x: 2, y: 2, z: 4, core: 2. Of those that a mesh axis runs over, the one named last changes fastest.
Arguments:
- model_field: float32 [16, 524288], P(None, ('groups', 'tile')), parts along dimension 1, may hold values from -6 to 6
- direction: float32 [16, 524288], P(None, ('groups', 'tile')), parts along dimension 1, may hold values from -100 to 100
- old_grad: float32 [16, 524288], P(None, ('groups', 'tile')), parts along dimension 1, may hold values from -100 to 100
- residual: float32 [16, 65536], P(None, ('groups', 'tile')), parts along dimension 1, may hold values from -6 to 6
- block_pairs: int32 [256, 8], P(('groups', 'tile')), parts along dimension 0, may hold values from 0 to 159, as said below
- depth_band: int32 [524288], P(('groups', 'tile')), parts along dimension 0, may hold values from 0 to 15
- station_offsets: float32 [2, 65536], P(None, ('groups', 'tile')), parts along dimension 1, may hold values from -1.25 to 2.25, as said below
Outputs:
- new_model: float32 [16, 524288], P(None, ('groups', 'tile')), parts along dimension 1
- new_residual: float32 [16, 65536], P(None, ('groups', 'tile')), parts along dimension 1
- new_direction: float32 [16, 524288], P(None, ('groups', 'tile')), parts along dimension 1
The draws below stay inside these ranges and needn't reach their ends.
There are 2 independent parts, one for each index of `groups`. The reference program is written for one: setup_inputs(seed, part) draws one part's arguments, and reference() takes and returns one part's arrays. A program takes and returns all parts, laid end to end along the dimension named above; each array names one. Nothing has to cross between parts.
Inputs may be any that keep to these rules, and one draw needn't show every extreme that they name: `block_pairs`: each row lists 8 different codes. `station_offsets`: row 1 (along) lies between 0 and 1.
All inputs are finite; a program needn't handle non-finite values.
Results may differ from the reference program's by a relative error of at most 0.0003.
Values sent between devices are 32-bit elements; how exact they have to be, the bound alone decides.
A program may use at most 128 MiB of HBM per device.

```python
import math
import jax
import jax.numpy as jnp
from jax import lax

E = 16
C_DEV = 16384
S_DEV = 2048
CBLOCK = 512
SBLOCK = 256
PAIRS = 8
REACH = 2
BANDS = 16
COL_SIDE = 32
CELLS = 262144
STATIONS = 32768
PAIR_ROWS = 128
CODES = 160
N_TILE = 16


def spread_field(key, ceiling):
    key_rows, key_values = jax.random.split(key, 2)
    row_scale = jnp.exp(jax.random.uniform(key_rows, (E, 1), jnp.float32) * math.log(ceiling))
    position = jnp.arange(CELLS, dtype=jnp.int32).astype(jnp.float32)[None, :] / CELLS
    column_scale = jnp.exp(position * math.log(ceiling))
    own_part = jnp.clip(jax.random.normal(key_values, (E, CELLS), jnp.float32), -6.0, 6.0)
    return own_part * row_scale * column_scale / ceiling


def draw_direction(key, part):
    return spread_field(jax.random.fold_in(key, 11), 10.0)


def draw_old_grad(key, part):
    return spread_field(jax.random.fold_in(key, 23), 10.0)


def draw_block_pairs(key, part):
    code_ids = jnp.arange(CODES, dtype=jnp.int32)[None, :]
    row_ids = jnp.arange(PAIR_ROWS, dtype=jnp.int32)[:, None]
    scores = jax.random.randint(jax.random.fold_in(key, 37), (PAIR_ROWS, CODES), 0, 1 << 20, dtype=jnp.int32) * CODES + code_ids
    chosen = jnp.logical_and(row_ids == PAIR_ROWS // 2, jnp.logical_or(code_ids == 0, code_ids == CODES - 1))
    scores = scores + jnp.where(chosen, (1 << 21) * CODES, 0)
    ordered = jnp.argsort(-scores, axis=1)
    return ordered[:, :PAIRS].astype(jnp.int32)


def draw_station_offsets(key, part):
    key_across, key_along = jax.random.split(jax.random.fold_in(key, 41))
    across = jax.random.uniform(key_across, (STATIONS,), jnp.float32) * 3.5 - 1.25
    along = jax.random.uniform(key_along, (STATIONS,), jnp.float32)
    return jnp.stack([across, along], axis=0)


def place_ends(array, key, smallest, high):
    longest = array.shape.index(max(array.shape))
    spots = []
    for shift in (0, 1):
        where = [jax.random.randint(jax.random.fold_in(key, axis), (), 0, length) for axis, length in enumerate(array.shape)]
        where[longest] = (where[longest] + shift) % array.shape[longest]
        spots.append(tuple(where))
    return array.at[spots[0]].set(smallest).at[spots[1]].set(high)


def steps_of(stream_key, extent, cuts, low, high):
    level = 1.0
    for axis_at, blocks in cuts:
        steps = jax.random.uniform(jax.random.fold_in(jax.random.fold_in(stream_key, 6), axis_at), (blocks,), jnp.float32, low / len(cuts), high / len(cuts))
        level = level * jnp.repeat(jnp.exp(steps), extent[axis_at] // blocks).reshape((-1,) + (1,) * (len(extent) - 1 - axis_at))
    return level


def gaussian(stream_key, shape, width, bound, cuts=(), held_as=jnp.bfloat16):
    array = width * jax.random.normal(stream_key, shape, jnp.float32)
    if cuts:
        array = array * steps_of(stream_key, shape, cuts, -0.22, 0.18)
    return jnp.clip(array, -bound, bound).astype(held_as)


def setup_inputs(seed: int = 0, part: int = 0) -> dict:
    streams_of = jax.random.split(jax.random.key(seed), 8)
    own_keys = jax.random.split(jax.random.fold_in(streams_of[7], part), 8)
    return {
        "model_field": gaussian(own_keys[0], (E, CELLS), 1.0, 6.0, ((1, 16),), jnp.float32),
        "direction": draw_direction(jax.random.fold_in(jax.random.fold_in(streams_of[7], part), 71), part),
        "old_grad": draw_old_grad(jax.random.fold_in(jax.random.fold_in(streams_of[7], part), 71), part),
        "residual": gaussian(own_keys[3], (E, STATIONS), 1.0, 6.0, ((1, 16),), jnp.float32),
        "block_pairs": draw_block_pairs(jax.random.fold_in(jax.random.fold_in(streams_of[7], part), 71), part),
        "depth_band": place_ends(jax.random.randint(own_keys[5], (CELLS,), 0, BANDS), jax.random.fold_in(own_keys[5], 1), 0, BANDS - 1).astype(jnp.int32),
        "station_offsets": draw_station_offsets(jax.random.fold_in(jax.random.fold_in(streams_of[7], part), 71), part),
    }


HIGHEST = lax.Precision.HIGHEST
DEPTH_RANGE = 2.0
DEPTH_SHIFT = 0.25
DAMPING = 1.0
GUARD = 1e-06

def point_kernel(station_across, station_along, cell_across, cell_along, cell_depth):
    across_gap = station_across[..., :, None] - cell_across[..., None, :]
    along_gap = station_along[..., :, None] - cell_along[..., None, :]
    depth_column = cell_depth[..., None, :]
    inverse = lax.rsqrt(across_gap * across_gap + along_gap * along_gap + depth_column * depth_column)
    return depth_column * inverse * inverse * inverse

def reference(model_field, direction, old_grad, residual, block_pairs, depth_band, station_offsets):
    cell_index = jnp.arange(CELLS, dtype=jnp.int32)
    column = cell_index % C_DEV % (COL_SIDE * COL_SIDE)
    cell_across = ((column % COL_SIDE).astype(jnp.float32) + 0.5) / COL_SIDE + (cell_index // C_DEV).astype(jnp.float32)
    cell_along = ((column // COL_SIDE).astype(jnp.float32) + 0.5) / COL_SIDE
    cell_depth = (depth_band.astype(jnp.float32) + 0.5) * (DEPTH_RANGE / BANDS)
    weight = (cell_depth + DEPTH_SHIFT) ** 1.5
    station_index = jnp.arange(STATIONS, dtype=jnp.int32)
    station_across = station_offsets[0] + (station_index // S_DEV).astype(jnp.float32)
    station_along = station_offsets[1]
    kernel_scale = 2.0 / math.sqrt(C_DEV)
    cell_blocks = C_DEV // CBLOCK
    block_rows = jnp.arange(PAIR_ROWS, dtype=jnp.int32)

    def block_matrix(row_id, code_value):
        tile_id = row_id // (S_DEV // SBLOCK)
        target = tile_id + code_value // cell_blocks - REACH
        inside = jnp.logical_and(target >= 0, target < N_TILE).astype(jnp.float32)
        cell_start = (jnp.clip(target, 0, N_TILE - 1) * C_DEV + code_value % cell_blocks * CBLOCK).astype(jnp.int32)
        station_start = (row_id * SBLOCK).astype(jnp.int32)
        matrix = point_kernel(lax.dynamic_slice_in_dim(station_across, station_start, SBLOCK), lax.dynamic_slice_in_dim(station_along, station_start, SBLOCK), lax.dynamic_slice_in_dim(cell_across, cell_start, CBLOCK), lax.dynamic_slice_in_dim(cell_along, cell_start, CBLOCK), lax.dynamic_slice_in_dim(cell_depth, cell_start, CBLOCK))
        return (matrix * (kernel_scale * inside), cell_start)
    weighted = weight[None, :] * direction

    def forward_row(row_id):

        def add_pair(running, code_value):
            built = block_matrix(row_id, code_value)
            values = lax.dynamic_slice_in_dim(weighted, built[1], CBLOCK, 1)
            return (running + jnp.dot(values, built[0].T, precision=HIGHEST, preferred_element_type=jnp.float32), None)
        result, unused = lax.scan(add_pair, jnp.zeros((E, SBLOCK), jnp.float32), block_pairs[row_id])
        return result
    image_blocks = lax.map(forward_row, block_rows)
    image_data = jnp.transpose(image_blocks, (1, 0, 2)).reshape(E, STATIONS)

    def adjoint(values):

        def per_row(accumulated, row_id):
            station_values = lax.dynamic_slice_in_dim(values, (row_id * SBLOCK).astype(jnp.int32), SBLOCK, 1)

            def add_pair(running, code_value):
                built = block_matrix(row_id, code_value)
                contribution = jnp.dot(station_values, built[0], precision=HIGHEST, preferred_element_type=jnp.float32)
                current = lax.dynamic_slice_in_dim(running, built[1], CBLOCK, 1)
                return (lax.dynamic_update_slice_in_dim(running, current + contribution, built[1], 1), None)
            accumulated, unused = lax.scan(add_pair, accumulated, block_pairs[row_id])
            return (accumulated, None)
        accumulated, unused = lax.scan(per_row, jnp.zeros((E, CELLS), jnp.float32), block_rows)
        return weight[None, :] * accumulated
    gamma_old = jnp.sum(old_grad * old_grad)
    curvature = jnp.sum(image_data * image_data) + DAMPING * jnp.sum(direction * direction)
    step_length = gamma_old / (curvature + GUARD)
    new_model = model_field + step_length * direction
    new_residual = residual - step_length * image_data
    gradient = adjoint(new_residual) - DAMPING * new_model
    gamma_new = jnp.sum(gradient * gradient)
    new_direction = gradient + gamma_new / (gamma_old + GUARD) * direction
    return (new_model, new_residual, new_direction)
```

```python
import functools
import math

import jax
import jax.numpy as jnp
from jax import lax
from jax.experimental import pallas as pl
from jax.experimental.pallas import tpu as pltpu
from jax.sharding import PartitionSpec as P

CBLOCK = 512
SBLOCK = 256
REACH = 2
BANDS = 16
COL_SIDE = 32
DEPTH_RANGE = 2.0
DEPTH_SHIFT = 0.25
DAMPING = 1.0
GUARD = 1e-06

SPAN = 2 * REACH + 1
HOPS = tuple(r for r in range(-REACH, REACH + 1) if r != 0)
UNROLL = 8
KEPT = 88
MESH = pl.DeviceIdType.MESH
F32 = jnp.float32
BF16 = jnp.bfloat16
VMEM_LIMIT = 6 * 1024 * 1024


def exists(me, r, n):
    return jnp.logical_and(me + r >= 0, me + r < n)


def split(x):
    high = x.astype(BF16)
    return high, (x - high.astype(F32)).astype(BF16)


def lane_sums(x):
    total = jnp.sum(x, axis=0, keepdims=True)
    out = total[:, 0:128]
    for k in range(1, x.shape[1] // 128):
        out = out + total[:, k * 128 : (k + 1) * 128]
    return out


def exchange_kernel(
    n, scale, blocks, dirn, pairs, band, offs,
    st_o, codes_o, v_o, f_o, z_o, norm_o, send_sem, recv_sem,
):
    me = lax.axis_index("tile")
    rows = pairs.shape[0]
    barrier = pltpu.get_barrier_semaphore()
    for r in HOPS:
        @pl.when(exists(me, r, n))
        def _():
            pl.semaphore_signal(barrier, inc=1, device_id={"tile": me + r}, device_id_type=MESH)

    own = REACH * rows
    for k in range(rows):
        st_o[own + k] = offs[:, k * SBLOCK : (k + 1) * SBLOCK]
    codes_o[REACH] = pairs[...]
    for r in HOPS:
        @pl.when(jnp.logical_not(exists(me, r, n)))
        def _():
            t = r + REACH
            st_o[t * rows : (t + 1) * rows] = jnp.zeros((rows,) + st_o.shape[1:], F32)
            codes_o[t] = jnp.full(codes_o.shape[1:], -1, jnp.int32)

    peers = sum(exists(me, r, n).astype(jnp.int32) for r in HOPS)
    pl.semaphore_wait(barrier, peers)

    def copies(q, r):
        t = REACH - r
        made = []
        for which, (src, dst) in enumerate((
            (codes_o.at[REACH], codes_o.at[t]),
            (st_o.at[pl.ds(own, rows)], st_o.at[pl.ds(t * rows, rows)]),
        )):
            made.append(pltpu.make_async_remote_copy(
                src_ref=src, dst_ref=dst, send_sem=send_sem.at[which, q],
                recv_sem=recv_sem.at[which, q], device_id={"tile": me + r}, device_id_type=MESH,
            ))
        return made

    for q, r in enumerate(HOPS):
        @pl.when(exists(me, r, n))
        def _():
            for one in copies(q, r):
                one.start()

    depth = (band[...].astype(F32) + 0.5) * (DEPTH_RANGE / BANDS)
    shifted = depth + DEPTH_SHIFT
    f_o[...] = scale * depth * (shifted * jnp.sqrt(shifted))
    z_o[...] = (depth * depth).T

    def block(b, total):
        for q in range(CBLOCK // 128):
            lanes = pl.ds(pl.multiple_of(b * CBLOCK + q * 128, 128), 128)
            values = dirn[:, lanes]
            high, low = split(f_o[pl.ds(b * (CBLOCK // 128) + q, 1), :] * values)
            v_o[b, 0:16, q * 128 : (q + 1) * 128] = high
            v_o[b, 16:32, q * 128 : (q + 1) * 128] = low
            total = total + values * values
        return total

    total = lax.fori_loop(0, blocks, block, jnp.zeros((dirn.shape[0], 128), F32))
    norm_o[...] = jnp.concatenate(
        [jnp.zeros((1, 128), F32), lane_sums(total), jnp.zeros((6, 128), F32)], axis=0
    )

    for q, r in enumerate(HOPS):
        @pl.when(exists(me, r, n))
        def _():
            for one in copies(q, r):
                one.wait_send()

        @pl.when(exists(me, -r, n))
        def _():
            for one in copies(q, r):
                one.wait_recv()


def kernel_halves(entry, st, z):
    j = lax.shift_right_logical(entry, 5)
    b = lax.bitwise_and(entry, 31)
    at = jnp.minimum(j, st.shape[0] - 1)
    rows = st.shape[0] // SPAN
    moved = (at // rows - REACH).astype(F32)
    parity = lax.bitwise_and(b, 1).astype(F32)
    place = st[at]
    sx = place[0:1, :] + moved
    sy = place[1:2, :] - 0.5 * parity
    column = (lax.broadcasted_iota(jnp.int32, (COL_SIDE, SBLOCK), 0).astype(F32) + 0.5) / COL_SIDE
    across = sx - column
    across = across * across
    which = jnp.full((COL_SIDE, 128), b * (CBLOCK // 128), jnp.int32)
    halves = []
    for h in range(2):
        highs, lows = [], []
        for a in range(h * 8, h * 8 + 8):
            along = sy - (a + 0.5) / COL_SIDE
            along = along * along
            low_row = a % 4 * COL_SIDE
            picked = jnp.take_along_axis(z[low_row : low_row + COL_SIDE, :], which + a // 4, axis=1)
            picked = jnp.concatenate([picked, picked], axis=1)
            inverse = lax.rsqrt(across + (along + picked))
            high, low = split(inverse * inverse * inverse)
            highs.append(high)
            lows.append(low)
        halves.append((jnp.concatenate(highs, axis=0), jnp.concatenate(lows, axis=0)))
    return j, b, halves


def forward_kernel(codes, st, z, v, img, pair_list, count, *kept):
    rows = codes.shape[1]
    img[...] = jnp.zeros(img.shape, F32)
    filled = jnp.int32(0)
    for t in range(SPAN):
        def pick(row, filled):
            for p in range(codes.shape[2]):
                code = codes[t, row, p]
                pair_list[filled] = (t * rows + row) * 32 + lax.bitwise_and(code, 31)
                hit = lax.shift_right_arithmetic(code, 5) == SPAN - 1 - t
                filled = filled + hit.astype(jnp.int32)
            return filled
        filled = lax.fori_loop(0, rows, pick, filled)
    for u in range(UNROLL):
        pair_list[filled + u] = SPAN * rows * 32
    steps = (filled + (UNROLL - 1)) // UNROLL
    count[0] = steps
    count[1] = jnp.minimum(steps, KEPT // UNROLL)

    def step(keep, i, carry):
        for u in range(UNROLL):
            j, b, halves = kernel_halves(pair_list[i * UNROLL + u], st, z)
            out = jnp.zeros((32, SBLOCK), F32)
            for h in range(2):
                values = v[b, :, h * 256 : (h + 1) * 256]
                for w, part in enumerate(halves[h]):
                    if keep:
                        kept[u][i, h, w] = part
                    out = out + jnp.dot(values, part, preferred_element_type=F32)
            img[j] += out[0:16] + out[16:32]
        return carry

    lax.fori_loop(0, count[1], functools.partial(step, True), 0)
    lax.fori_loop(count[1], steps, functools.partial(step, False), 0)


def all_sum(n, me, mine, landing, send_sem, recv_sem, start, finish):
    def made(k):
        return pltpu.make_async_remote_copy(
            src_ref=mine, dst_ref=landing.at[k], send_sem=send_sem.at[k], recv_sem=recv_sem.at[k],
            device_id={"tile": lax.rem(me + k, n)}, device_id_type=MESH,
        )
    if start:
        def go(k, c):
            made(k).start()
            return c
        lax.fori_loop(1, n, go, 0)
    if finish:
        def done(k, c):
            made(k).wait()
            return c
        lax.fori_loop(1, n, done, 0)


def greet_all(n, me):
    barrier = pltpu.get_barrier_semaphore()

    def greet(k, c):
        pl.semaphore_signal(
            barrier, inc=1, device_id={"tile": lax.rem(me + k, n)}, device_id_type=MESH
        )
        return c
    lax.fori_loop(1, n, greet, 0)
    pl.semaphore_wait(barrier, n - 1)


def image_kernel(
    n, rows, img, res, norm, old, newres_o, scal_o,
    transit, joined, part_rx, norm_tx, norm_rx, send_sem, recv_sem, nsend_sem, nrecv_sem,
):
    me = lax.axis_index("tile")
    greet_all(n, me)
    s = 1 - 2 * lax.rem(me, 2)
    outward = exists(me, -2 * s, n)
    inward = exists(me, 2 * s, n)

    def slab(ref, r):
        return ref.at[pl.ds((REACH + r) * rows, rows)]

    def copy(number, src, dst, to):
        return pltpu.make_async_remote_copy(
            src_ref=src, dst_ref=dst, send_sem=send_sem.at[number],
            recv_sem=recv_sem.at[number], device_id={"tile": to}, device_id_type=MESH,
        )

    to_join = copy(0, slab(img, 2 * s), transit, me + s)
    to_sibling = copy(1, slab(img, s), part_rx.at[0], me + s)
    to_far = copy(2, slab(img, -2 * s), part_rx.at[1], me - 2 * s)
    to_near = copy(3, joined, part_rx.at[2], me - s)
    own = slab(newres_o, 0)
    give_near = copy(4, own, slab(newres_o, s), me - s)
    give_far = copy(5, own, slab(newres_o, -2 * s), me + 2 * s)
    give_sibling = copy(6, own, slab(newres_o, -s), me + s)
    pass_on = copy(7, slab(newres_o, -s), slab(newres_o, -2 * s), me + s)

    @pl.when(inward)
    def _():
        to_join.start()

    @pl.when(outward)
    def _():
        to_far.start()
    to_sibling.start()

    def squares(k, total):
        values = old[:, pl.ds(pl.multiple_of(k * 512, 512), 512)]
        return total + values * values

    before = lax.fori_loop(0, old.shape[1] // 512, squares, jnp.zeros((old.shape[0], 512), F32))
    norm_tx[...] = norm[...]
    norm_tx[0:1, :] = lane_sums(before)

    @pl.when(outward)
    def _():
        to_join.wait_recv()
        joined[...] = transit[...] + img[pl.ds((REACH - s) * rows, rows)]
        to_near.start()

    to_sibling.wait_recv()
    here = REACH * rows
    newres_o[here : here + rows] = img[here : here + rows] + part_rx[0]

    @pl.when(inward)
    def _():
        to_far.wait_recv()
        newres_o[here : here + rows] += part_rx[1]

    @pl.when(outward)
    def _():
        to_near.wait_recv()
        newres_o[here : here + rows] += part_rx[2]

    image = newres_o[here : here + rows]
    norm_tx[2:3, :] = lane_sums(jnp.sum(image * image, axis=0))
    all_sum(n, me, norm_tx, norm_rx, nsend_sem, nrecv_sem, True, True)
    norm_rx[0] = norm_tx[...]
    totals = jnp.sum(jnp.sum(norm_rx[...], axis=0), axis=1, keepdims=True)
    gamma_old = totals[0:1]
    length = gamma_old / (totals[2:3] + DAMPING * totals[1:2] + GUARD)
    scal_o[...] = jnp.concatenate(
        [jnp.broadcast_to(length, (4, 128)), jnp.broadcast_to(gamma_old, (4, 128))], axis=0
    )
    for k in range(rows):
        newres_o[here + k] = res[:, k * SBLOCK : (k + 1) * SBLOCK] - length * newres_o[here + k]

    @pl.when(outward)
    def _():
        give_near.start()

    @pl.when(inward)
    def _():
        give_far.start()
    give_sibling.start()

    @pl.when(outward)
    def _():
        give_near.wait_recv()
        pass_on.start()
        to_far.wait_send()
        to_near.wait_send()
        give_far.wait_recv()
        give_near.wait_send()
        pass_on.wait_send()

    @pl.when(inward)
    def _():
        to_join.wait_send()
        give_far.wait_send()
        pass_on.wait_recv()
    to_sibling.wait_send()
    give_sibling.wait()


def adjoint_kernel(
    pair_list, count, st, z, f, newres, scal, model, dirn, *rest,
):
    kept = rest[:UNROLL]
    model_hbm, grad_o, gamma_o, res_o, acc, parts, model_o, out_sem = rest[UNROLL:]
    slots = newres.shape[0]
    rows = slots // SPAN
    for k in range(rows):
        res_o[:, k * SBLOCK : (k + 1) * SBLOCK] = newres[REACH * rows + k]

    length = scal[0:1, 0:1]

    def update(b, c):
        lanes = pl.ds(pl.multiple_of(b * CBLOCK, CBLOCK), CBLOCK)
        model_o[:, lanes] = model[:, lanes] + length * dirn[:, lanes]
        return c
    lax.fori_loop(0, acc.shape[0], update, 0)
    leave = pltpu.make_async_copy(model_o, model_hbm, out_sem)
    leave.start()

    def cut(k, c):
        high, low = split(newres[k])
        parts[k, 0:16, :] = high
        parts[k, 16:32, :] = low
        return c
    lax.fori_loop(0, slots, cut, 0)
    parts[slots] = jnp.zeros((32, SBLOCK), BF16)
    acc[...] = jnp.zeros(acc.shape, F32)

    def add_pair(j, b, halves):
        values = parts[j]
        for h in range(2):
            out = jnp.zeros((32, 256), F32)
            for part in halves[h]:
                out = out + lax.dot_general(
                    values, part, (((1,), (1,)), ((), ())), preferred_element_type=F32
                )
            acc[b, :, h * 256 : (h + 1) * 256] += out[0:16] + out[16:32]

    def reread(i, carry):
        for u in range(UNROLL):
            entry = pair_list[i * UNROLL + u]
            halves = [[kept[u][i, h, w] for w in range(2)] for h in range(2)]
            add_pair(lax.shift_right_logical(entry, 5), lax.bitwise_and(entry, 31), halves)
        return carry

    def rebuild(i, carry):
        for u in range(UNROLL):
            add_pair(*kernel_halves(pair_list[i * UNROLL + u], st, z))
        return carry

    lax.fori_loop(0, count[1], reread, 0)
    lax.fori_loop(count[1], count[0], rebuild, 0)

    def finish(b, total):
        lanes = pl.ds(pl.multiple_of(b * CBLOCK, CBLOCK), CBLOCK)
        new_model = model_o[:, lanes]
        factor = jnp.concatenate(
            [f[pl.ds(b * (CBLOCK // 128) + q, 1), :] for q in range(CBLOCK // 128)], axis=1
        )
        gradient = factor * acc[b] - DAMPING * new_model
        grad_o[:, lanes] = gradient
        return total + gradient * gradient

    total = lax.fori_loop(0, acc.shape[0], finish, jnp.zeros((model.shape[0], CBLOCK), F32))
    gamma_o[...] = jnp.concatenate([lane_sums(total), jnp.zeros((7, 128), F32)], axis=0)
    leave.wait()


def gamma_kernel(n, gamma, scal, ratio_o, landing, send_sem, recv_sem):
    me = lax.axis_index("tile")
    greet_all(n, me)
    all_sum(n, me, gamma, landing, send_sem, recv_sem, True, True)
    landing[0] = gamma[...]
    total = jnp.sum(jnp.sum(landing[...], axis=0), axis=1, keepdims=True)[0:1]
    ratio_o[...] = total / (scal[4:5, 0:1] + GUARD)


def shards(model_field, direction, old_grad, residual, block_pairs, depth_band, station_offsets):
    n = lax.axis_size("tile")
    epochs, cells = model_field.shape
    stations = residual.shape[1]
    rows = block_pairs.shape[0]
    pairs = block_pairs.shape[1]
    blocks = cells // CBLOCK
    scale = 2.0 / math.sqrt(cells)
    vmem = pl.BlockSpec(memory_space=pltpu.VMEM)
    smem = pl.BlockSpec(memory_space=pltpu.SMEM)
    shape = jax.ShapeDtypeStruct
    slots = SPAN * rows
    dma = pltpu.SemaphoreType.DMA

    def params(number=None):
        if number is None:
            return pltpu.CompilerParams(vmem_limit_bytes=VMEM_LIMIT)
        return pltpu.CompilerParams(
            vmem_limit_bytes=VMEM_LIMIT, collective_id=number, has_side_effects=True
        )

    st, codes, v, f, z, norm = pl.pallas_call(
        functools.partial(exchange_kernel, n, scale, blocks),
        out_shape=(
            shape((slots, 2, SBLOCK), F32),
            shape((SPAN, rows, pairs), jnp.int32),
            shape((blocks, 2 * epochs, CBLOCK), BF16),
            shape((cells // 128, 128), F32),
            shape((128, cells // 128), F32),
            shape((8, 128), F32),
        ),
        in_specs=[vmem] * 4,
        out_specs=(vmem,) * 6,
        scratch_shapes=[
            dma((2, len(HOPS))),
            dma((2, len(HOPS))),
        ],
        compiler_params=params(0),
        name="exchange",
    )(direction, block_pairs, depth_band.reshape(cells // 128, 128), station_offsets)

    img, pair_list, count, *kept = pl.pallas_call(
        forward_kernel,
        out_shape=(
            shape((slots + 1, epochs, SBLOCK), F32),
            shape((slots * pairs + UNROLL,), jnp.int32),
            shape((2,), jnp.int32),
        ) + (pltpu.VMEM((KEPT // UNROLL, 2, 2, 256, SBLOCK), BF16),) * UNROLL,
        in_specs=[smem, vmem, vmem, vmem],
        out_specs=(vmem, smem, smem) + (vmem,) * UNROLL,
        compiler_params=params(),
        name="forward",
    )(codes, st, z, v)

    kept = [pltpu.with_memory_space_constraint(k, pltpu.VMEM) for k in kept]
    newres, scal = pl.pallas_call(
        functools.partial(image_kernel, n, rows),
        out_shape=(shape((slots, epochs, SBLOCK), F32), shape((8, 128), F32)),
        in_specs=[vmem] * 4,
        out_specs=(vmem,) * 2,
        scratch_shapes=[
            pltpu.VMEM((rows, epochs, SBLOCK), F32),
            pltpu.VMEM((rows, epochs, SBLOCK), F32),
            pltpu.VMEM((3, rows, epochs, SBLOCK), F32),
            pltpu.VMEM((8, 128), F32),
            pltpu.VMEM((n, 8, 128), F32),
            dma((8,)),
            dma((8,)),
            dma((n,)),
            dma((n,)),
        ],
        compiler_params=params(1),
        name="images",
    )(img, residual, norm, old_grad)

    new_model, gradient, gamma, new_residual = pl.pallas_call(
        adjoint_kernel,
        out_shape=(
            shape((epochs, cells), F32),
            shape((epochs, cells), F32),
            shape((8, 128), F32),
            shape((epochs, stations), F32),
        ),
        in_specs=[smem, smem] + [vmem] * (7 + UNROLL),
        out_specs=(pl.BlockSpec(memory_space=pltpu.HBM),) + (vmem,) * 3,
        scratch_shapes=[
            pltpu.VMEM((blocks, epochs, CBLOCK), F32),
            pltpu.VMEM((slots + 1, 2 * epochs, SBLOCK), BF16),
            pltpu.VMEM((epochs, cells), F32),
            dma(()),
        ],
        compiler_params=params(),
        name="adjoint",
    )(pair_list, count, st, z, f, newres, scal, model_field, direction, *kept)

    ratio = pl.pallas_call(
        functools.partial(gamma_kernel, n),
        out_shape=shape((1, 1), F32),
        in_specs=[vmem] * 2,
        out_specs=vmem,
        scratch_shapes=[pltpu.VMEM((n, 8, 128), F32), dma((n,)), dma((n,))],
        compiler_params=params(2),
        name="gamma",
    )(gamma, scal)
    new_direction = gradient + ratio.reshape(()) * direction
    return (new_model, new_residual, new_direction)


def solution(mesh):
    both = ("groups", "tile")
    wide = P(None, both)
    return jax.shard_map(
        shards,
        mesh=mesh,
        in_specs=(wide, wide, wide, wide, P(both, None), P(both), wide),
        out_specs=(wide, wide, wide),
        check_vma=False,
    )
```

```python
import functools
import math

import jax
import jax.numpy as jnp
from jax import lax
from jax.experimental import pallas as pl
from jax.experimental.pallas import tpu as pltpu
from jax.sharding import PartitionSpec as P

CBLOCK = 512
SBLOCK = 256
REACH = 2
BANDS = 16
COL_SIDE = 32
DEPTH_RANGE = 2.0
DEPTH_SHIFT = 0.25
DAMPING = 1.0
GUARD = 1e-06

SPAN = 2 * REACH + 1
CHUNKS = 4
HOPS = tuple(r for r in range(-REACH, REACH + 1) if r != 0)
UNROLL = 4
MESH = pl.DeviceIdType.MESH
F32 = jnp.float32
BF16 = jnp.bfloat16
VMEM_LIMIT = 48 * 1024 * 1024


def exists(me, r, n):
    return jnp.logical_and(me + r >= 0, me + r < n)


def split(x):
    high = x.astype(BF16)
    return high, (x - high.astype(F32)).astype(BF16)


def lane_sums(x):
    total = jnp.sum(x, axis=0, keepdims=True)
    out = total[:, 0:128]
    for k in range(1, x.shape[1] // 128):
        out = out + total[:, k * 128 : (k + 1) * 128]
    return out


def exchange_kernel(
    n, scale, blocks, dirn_hbm, pairs, band_hbm, offs_hbm,
    st_o, codes_o, v_o, f_o, z_o, norm_o,
    dirn, band, offs, in_sem, send_sem, recv_sem,
):
    me = lax.axis_index("tile")
    rows = pairs.shape[0]
    part = dirn.shape[1] // CHUNKS
    fetch_offs = pltpu.make_async_copy(offs_hbm, offs, in_sem.at[0])
    fetch_pairs = pltpu.make_async_copy(pairs, codes_o.at[REACH], in_sem.at[1])
    fetch_band = pltpu.make_async_copy(band_hbm, band, in_sem.at[2])
    fetch_dirn = [
        pltpu.make_async_copy(
            dirn_hbm.at[:, k * part : (k + 1) * part],
            dirn.at[:, k * part : (k + 1) * part],
            in_sem.at[3 + k],
        )
        for k in range(CHUNKS)
    ]
    for one in [fetch_offs, fetch_pairs, fetch_band] + fetch_dirn:
        one.start()
    barrier = pltpu.get_barrier_semaphore()
    for r in HOPS:
        @pl.when(exists(me, r, n))
        def _():
            pl.semaphore_signal(barrier, inc=1, device_id={"tile": me + r}, device_id_type=MESH)

    own = REACH * rows
    for r in HOPS:
        @pl.when(jnp.logical_not(exists(me, r, n)))
        def _():
            t = r + REACH
            st_o[t * rows : (t + 1) * rows] = jnp.zeros((rows,) + st_o.shape[1:], F32)
            codes_o[t] = jnp.full(codes_o.shape[1:], -1, jnp.int32)
    fetch_offs.wait()
    for k in range(rows):
        st_o[own + k] = offs[:, k * SBLOCK : (k + 1) * SBLOCK]
    fetch_pairs.wait()

    peers = sum(exists(me, r, n).astype(jnp.int32) for r in HOPS)
    pl.semaphore_wait(barrier, peers)

    def copies(q, r):
        t = REACH - r
        made = []
        for which, (src, dst) in enumerate((
            (codes_o.at[REACH], codes_o.at[t]),
            (st_o.at[pl.ds(own, rows)], st_o.at[pl.ds(t * rows, rows)]),
        )):
            made.append(pltpu.make_async_remote_copy(
                src_ref=src, dst_ref=dst, send_sem=send_sem.at[which, q],
                recv_sem=recv_sem.at[which, q], device_id={"tile": me + r}, device_id_type=MESH,
            ))
        return made

    for q, r in enumerate(HOPS):
        @pl.when(exists(me, r, n))
        def _():
            for one in copies(q, r):
                one.start()

    fetch_band.wait()
    depth = (band[...].astype(F32) + 0.5) * (DEPTH_RANGE / BANDS)
    shifted = depth + DEPTH_SHIFT
    f_o[...] = scale * depth * (shifted * jnp.sqrt(shifted))
    z_o[...] = (depth * depth).T

    def block(b, total):
        for q in range(CBLOCK // 128):
            lanes = pl.ds(pl.multiple_of(b * CBLOCK + q * 128, 128), 128)
            values = dirn[:, lanes]
            high, low = split(f_o[pl.ds(b * (CBLOCK // 128) + q, 1), :] * values)
            v_o[b, 0:16, q * 128 : (q + 1) * 128] = high
            v_o[b, 16:32, q * 128 : (q + 1) * 128] = low
            total = total + values * values
        return total

    total = jnp.zeros((dirn.shape[0], 128), F32)
    for k in range(CHUNKS):
        fetch_dirn[k].wait()
        total = lax.fori_loop(k * blocks // CHUNKS, (k + 1) * blocks // CHUNKS, block, total)
    norm_o[...] = jnp.broadcast_to(lane_sums(total), norm_o.shape)

    for q, r in enumerate(HOPS):
        @pl.when(exists(me, r, n))
        def _():
            for one in copies(q, r):
                one.wait_send()

        @pl.when(exists(me, -r, n))
        def _():
            for one in copies(q, r):
                one.wait_recv()


def kernel_halves(entry, st, z):
    j = lax.shift_right_logical(entry, 5)
    b = lax.bitwise_and(entry, 31)
    at = jnp.minimum(j, st.shape[0] - 1)
    rows = st.shape[0] // SPAN
    moved = (at // rows - REACH).astype(F32)
    parity = lax.bitwise_and(b, 1).astype(F32)
    place = st[at]
    sx = jnp.broadcast_to(place[0:1, :] + moved, (8, SBLOCK))
    sy = jnp.broadcast_to(place[1:2, :] - 0.5 * parity, (8, SBLOCK))
    column = (lax.broadcasted_iota(jnp.int32, (COL_SIDE, SBLOCK), 0).astype(F32) + 0.5) / COL_SIDE
    across = jnp.concatenate([sx] * (COL_SIDE // 8), axis=0) - column
    across = across * across
    which = jnp.full((COL_SIDE, 128), b * (CBLOCK // 128), jnp.int32)
    halves = []
    for h in range(2):
        highs, lows = [], []
        for a in range(h * 8, h * 8 + 8):
            along = sy - (a + 0.5) / COL_SIDE
            along = jnp.concatenate([along * along] * (COL_SIDE // 8), axis=0)
            low_row = a % 4 * COL_SIDE
            picked = jnp.take_along_axis(z[low_row : low_row + COL_SIDE, :], which + a // 4, axis=1)
            picked = jnp.concatenate([picked, picked], axis=1)
            inverse = lax.rsqrt(across + (along + picked))
            high, low = split(inverse * inverse * inverse)
            highs.append(high)
            lows.append(low)
        halves.append((jnp.concatenate(highs, axis=0), jnp.concatenate(lows, axis=0)))
    return j, b, halves


def forward_kernel(codes, st, z, v, img, pair_list, count):
    rows = codes.shape[1]
    img[...] = jnp.zeros(img.shape, F32)
    filled = jnp.int32(0)
    for t in range(SPAN):
        def pick(row, filled):
            for p in range(codes.shape[2]):
                code = codes[t, row, p]
                pair_list[filled] = (t * rows + row) * 32 + lax.bitwise_and(code, 31)
                hit = lax.shift_right_arithmetic(code, 5) == SPAN - 1 - t
                filled = filled + hit.astype(jnp.int32)
            return filled
        filled = lax.fori_loop(0, rows, pick, filled)
    for u in range(UNROLL):
        pair_list[filled + u] = SPAN * rows * 32
    steps = (filled + (UNROLL - 1)) // UNROLL
    count[0] = steps

    def step(i, carry):
        for u in range(UNROLL):
            j, b, halves = kernel_halves(pair_list[i * UNROLL + u], st, z)
            out = jnp.zeros((32, SBLOCK), F32)
            for h in range(2):
                values = v[b, :, h * 256 : (h + 1) * 256]
                for part in halves[h]:
                    out = out + jnp.dot(values, part, preferred_element_type=F32)
            img[j] += out[0:16] + out[16:32]
        return carry

    lax.fori_loop(0, steps, step, 0)


def all_sum(n, me, mine, landing, send_sem, recv_sem, start, finish):
    def made(k):
        return pltpu.make_async_remote_copy(
            src_ref=mine, dst_ref=landing.at[k], send_sem=send_sem.at[k], recv_sem=recv_sem.at[k],
            device_id={"tile": lax.rem(me + k, n)}, device_id_type=MESH,
        )
    if start:
        def go(k, c):
            made(k).start()
            return c
        lax.fori_loop(1, n, go, 0)
    if finish:
        def done(k, c):
            made(k).wait()
            return c
        lax.fori_loop(1, n, done, 0)


def greet(n, me):
    barrier = pltpu.get_barrier_semaphore()

    def one(k, c):
        pl.semaphore_signal(
            barrier, inc=1, device_id={"tile": lax.rem(me + k, n)}, device_id_type=MESH
        )
        return c
    lax.fori_loop(1, n, one, 0)


def greeted(n):
    pl.semaphore_wait(pltpu.get_barrier_semaphore(), n - 1)


def image_kernel(
    n, rows, img, res, norm, old, newres_o, scal_o,
    transit, joined, part_rx, norm_tx, norm_rx, send_sem, recv_sem, nsend_sem, nrecv_sem,
):
    me = lax.axis_index("tile")
    greet(n, me)
    greeted(n)
    s = 1 - 2 * lax.rem(me, 2)
    outward = exists(me, -2 * s, n)
    inward = exists(me, 2 * s, n)

    def slab(ref, r):
        return ref.at[pl.ds((REACH + r) * rows, rows)]

    def copy(number, src, dst, to):
        return pltpu.make_async_remote_copy(
            src_ref=src, dst_ref=dst, send_sem=send_sem.at[number],
            recv_sem=recv_sem.at[number], device_id={"tile": to}, device_id_type=MESH,
        )

    to_join = copy(0, slab(img, 2 * s), transit, me + s)
    to_sibling = copy(1, slab(img, s), part_rx.at[0], me + s)
    to_far = copy(2, slab(img, -2 * s), part_rx.at[1], me - 2 * s)
    to_near = copy(3, joined, part_rx.at[2], me - s)
    own = slab(newres_o, 0)
    give_near = copy(4, own, slab(newres_o, s), me - s)
    give_far = copy(5, own, slab(newres_o, -2 * s), me + 2 * s)
    give_sibling = copy(6, own, slab(newres_o, -s), me + s)
    pass_on = copy(7, slab(newres_o, -s), slab(newres_o, -2 * s), me + s)

    @pl.when(inward)
    def _():
        to_join.start()

    @pl.when(outward)
    def _():
        to_far.start()
    to_sibling.start()

    def squares(k, total):
        values = old[:, pl.ds(pl.multiple_of(k * 512, 512), 512)]
        return total + values * values

    before = lax.fori_loop(0, old.shape[1] // 512, squares, jnp.zeros((old.shape[0], 512), F32))
    lane = lax.broadcasted_iota(jnp.int32, (1, 128), 1)
    gamma_part = jnp.sum(lane_sums(before), axis=1, keepdims=True)
    norm_part = DAMPING * jnp.sum(norm[0:1, :], axis=1, keepdims=True)
    known = jnp.where(lane == 0, gamma_part, jnp.where(lane == 1, norm_part, 0.0))

    @pl.when(outward)
    def _():
        to_join.wait_recv()
        joined[...] = transit[...] + img[pl.ds((REACH - s) * rows, rows)]
        to_near.start()

    to_sibling.wait_recv()
    here = REACH * rows
    newres_o[here : here + rows] = img[here : here + rows] + part_rx[0]

    @pl.when(inward)
    def _():
        to_far.wait_recv()
        newres_o[here : here + rows] += part_rx[1]

    @pl.when(outward)
    def _():
        to_near.wait_recv()
        newres_o[here : here + rows] += part_rx[2]

    image = newres_o[here : here + rows]
    squared = lane_sums(jnp.sum(image * image, axis=0))
    folded = squared + jnp.where(lane == 1, 0.0, pltpu.roll(jnp.where(lane < 2, squared, 0.0), 2, 1))
    norm_tx[...] = jnp.where(lane < 2, known, folded)
    all_sum(n, me, norm_tx, norm_rx, nsend_sem, nrecv_sem, True, True)
    norm_rx[0] = norm_tx[...]
    totals = jnp.sum(norm_rx[...], axis=0)
    gamma_old = jnp.sum(jnp.where(lane == 0, totals, 0.0), axis=1, keepdims=True)
    curvature = jnp.sum(jnp.where(lane == 0, 0.0, totals), axis=1, keepdims=True)
    length = gamma_old / (curvature + GUARD)
    scal_o[...] = jnp.concatenate(
        [jnp.broadcast_to(length, (4, 128)), jnp.broadcast_to(gamma_old, (4, 128))], axis=0
    )
    for k in range(rows):
        newres_o[here + k] = res[:, k * SBLOCK : (k + 1) * SBLOCK] - length * newres_o[here + k]

    @pl.when(outward)
    def _():
        give_near.start()

    @pl.when(inward)
    def _():
        give_far.start()
    give_sibling.start()

    @pl.when(outward)
    def _():
        give_near.wait_recv()
        pass_on.start()
        to_far.wait_send()
        to_near.wait_send()
        give_far.wait_recv()
        give_near.wait_send()
        pass_on.wait_send()

    @pl.when(inward)
    def _():
        to_join.wait_send()
        give_far.wait_send()
        pass_on.wait_recv()
    to_sibling.wait_send()
    give_sibling.wait()


def adjoint_kernel(
    pair_list, count, st, z, newres, scal, model, dirn,
    model_hbm, model_o, acc, res_o, parts, out_sem,
):
    slots = newres.shape[0]
    rows = slots // SPAN
    for k in range(rows):
        res_o[:, k * SBLOCK : (k + 1) * SBLOCK] = newres[REACH * rows + k]

    length = scal[0:1, 0:1]

    def update(b, c):
        lanes = pl.ds(pl.multiple_of(b * CBLOCK, CBLOCK), CBLOCK)
        model_o[:, lanes] = model[:, lanes] + length * dirn[:, lanes]
        return c
    lax.fori_loop(0, acc.shape[0], update, 0)
    leave = pltpu.make_async_copy(model_o, model_hbm, out_sem)
    leave.start()

    def cut(k, c):
        high, low = split(newres[k])
        parts[k, 0:16, :] = high
        parts[k, 16:32, :] = low
        return c
    lax.fori_loop(0, slots, cut, 0)
    parts[slots] = jnp.zeros((32, SBLOCK), BF16)
    acc[...] = jnp.zeros(acc.shape, F32)

    def step(i, carry):
        for u in range(UNROLL):
            j, b, halves = kernel_halves(pair_list[i * UNROLL + u], st, z)
            values = parts[j]
            for h in range(2):
                out = jnp.zeros((32, 256), F32)
                for part in halves[h]:
                    out = out + lax.dot_general(
                        values, part, (((1,), (1,)), ((), ())), preferred_element_type=F32
                    )
                acc[b, :, h * 256 : (h + 1) * 256] += out[0:16] + out[16:32]
        return carry

    lax.fori_loop(0, count[0], step, 0)

    leave.wait()


def gamma_kernel(n, acc, model, f, scal, grad_o, ratio_o, mine, landing, send_sem, recv_sem):
    me = lax.axis_index("tile")
    greet(n, me)

    def finish(b, total):
        lanes = pl.ds(pl.multiple_of(b * CBLOCK, CBLOCK), CBLOCK)
        factor = jnp.concatenate(
            [f[pl.ds(b * (CBLOCK // 128) + q, 1), :] for q in range(CBLOCK // 128)], axis=1
        )
        gradient = factor * acc[b] - DAMPING * model[:, lanes]
        grad_o[:, lanes] = gradient
        return total + gradient * gradient

    total = lax.fori_loop(0, acc.shape[0], finish, jnp.zeros((model.shape[0], CBLOCK), F32))
    mine[...] = lane_sums(total)
    greeted(n)
    all_sum(n, me, mine, landing, send_sem, recv_sem, True, True)
    landing[0] = mine[...]
    total = jnp.sum(jnp.sum(landing[...], axis=0), axis=1, keepdims=True)
    ratio_o[...] = total / (scal[4:5, 0:1] + GUARD)


def shards(model_field, direction, old_grad, residual, block_pairs, depth_band, station_offsets):
    n = lax.axis_size("tile")
    epochs, cells = model_field.shape
    stations = residual.shape[1]
    rows = block_pairs.shape[0]
    pairs = block_pairs.shape[1]
    blocks = cells // CBLOCK
    scale = 2.0 / math.sqrt(cells)
    vmem = pl.BlockSpec(memory_space=pltpu.VMEM)
    smem = pl.BlockSpec(memory_space=pltpu.SMEM)
    hbm = pl.BlockSpec(memory_space=pltpu.HBM)
    shape = jax.ShapeDtypeStruct
    slots = SPAN * rows
    dma = pltpu.SemaphoreType.DMA

    def params(number=None):
        if number is None:
            return pltpu.CompilerParams(vmem_limit_bytes=VMEM_LIMIT)
        return pltpu.CompilerParams(
            vmem_limit_bytes=VMEM_LIMIT, collective_id=number, has_side_effects=True
        )

    st, codes, v, f, z, norm = pl.pallas_call(
        functools.partial(exchange_kernel, n, scale, blocks),
        out_shape=(
            shape((slots, 2, SBLOCK), F32),
            shape((SPAN, rows, pairs), jnp.int32),
            shape((blocks, 2 * epochs, CBLOCK), BF16),
            shape((cells // 128, 128), F32),
            shape((128, cells // 128), F32),
            shape((8, 128), F32),
        ),
        in_specs=[hbm] * 4,
        out_specs=(vmem,) * 6,
        scratch_shapes=[
            pltpu.VMEM((epochs, cells), F32),
            pltpu.VMEM((cells // 128, 128), jnp.int32),
            pltpu.VMEM((2, stations), F32),
            dma((3 + CHUNKS,)),
            dma((2, len(HOPS))),
            dma((2, len(HOPS))),
        ],
        compiler_params=params(0),
        name="exchange",
    )(*(
        pltpu.with_memory_space_constraint(one, pltpu.HBM)
        for one in (direction, block_pairs, depth_band.reshape(cells // 128, 128), station_offsets)
    ))

    img, pair_list, count = pl.pallas_call(
        forward_kernel,
        out_shape=(
            shape((slots + 1, epochs, SBLOCK), F32),
            shape((slots * pairs + UNROLL,), jnp.int32),
            shape((1,), jnp.int32),
        ),
        in_specs=[smem, vmem, vmem, vmem],
        out_specs=(vmem, smem, smem),
        compiler_params=params(),
        name="forward",
    )(codes, st, z, v)

    newres, scal = pl.pallas_call(
        functools.partial(image_kernel, n, rows),
        out_shape=(shape((slots, epochs, SBLOCK), F32), shape((8, 128), F32)),
        in_specs=[vmem] * 4,
        out_specs=(vmem,) * 2,
        scratch_shapes=[
            pltpu.VMEM((rows, epochs, SBLOCK), F32),
            pltpu.VMEM((rows, epochs, SBLOCK), F32),
            pltpu.VMEM((3, rows, epochs, SBLOCK), F32),
            pltpu.VMEM((1, 128), F32),
            pltpu.VMEM((n, 1, 128), F32),
            dma((8,)),
            dma((8,)),
            dma((n,)),
            dma((n,)),
        ],
        compiler_params=params(1),
        name="images",
    )(img, residual, norm, old_grad)

    new_model, model_kept, acc, new_residual = pl.pallas_call(
        adjoint_kernel,
        out_shape=(
            shape((epochs, cells), F32),
            shape((epochs, cells), F32),
            shape((blocks, epochs, CBLOCK), F32),
            shape((epochs, stations), F32),
        ),
        in_specs=[smem, smem] + [vmem] * 6,
        out_specs=(hbm,) + (vmem,) * 3,
        scratch_shapes=[pltpu.VMEM((slots + 1, 2 * epochs, SBLOCK), BF16), dma(())],
        compiler_params=params(),
        name="adjoint",
    )(pair_list, count, st, z, newres, scal, model_field, direction)

    gradient, ratio = pl.pallas_call(
        functools.partial(gamma_kernel, n),
        out_shape=(shape((epochs, cells), F32), shape((1, 1), F32)),
        in_specs=[vmem] * 4,
        out_specs=(vmem,) * 2,
        scratch_shapes=[
            pltpu.VMEM((1, 128), F32), pltpu.VMEM((n, 1, 128), F32), dma((n,)), dma((n,)),
        ],
        compiler_params=params(2),
        name="gamma",
    )(acc, model_kept, f, scal)
    new_direction = gradient + ratio.reshape(()) * direction
    return (new_model, new_residual, new_direction)


def solution(mesh):
    both = ("groups", "tile")
    wide = P(None, both)
    return jax.shard_map(
        shards,
        mesh=mesh,
        in_specs=(wide, wide, wide, wide, P(both, None), P(both), wide),
        out_specs=(wide, wide, wide),
        check_vma=False,
    )
```

```python
import functools
import math

import jax
import jax.numpy as jnp
from jax import lax
from jax.experimental import pallas as pl
from jax.experimental.pallas import tpu as pltpu
from jax.sharding import PartitionSpec as P

CBLOCK = 512
SBLOCK = 256
REACH = 2
BANDS = 16
COL_SIDE = 32
DEPTH_RANGE = 2.0
DEPTH_SHIFT = 0.25
DAMPING = 1.0
GUARD = 1e-06

SPAN = 2 * REACH + 1
CHUNKS = 4
HOPS = tuple(r for r in range(-REACH, REACH + 1) if r != 0)
UNROLL = 8
MESH = pl.DeviceIdType.MESH
F32 = jnp.float32
BF16 = jnp.bfloat16
VMEM_LIMIT = 48 * 1024 * 1024


def exists(me, r, n):
    return jnp.logical_and(me + r >= 0, me + r < n)


def split(x):
    high = x.astype(BF16)
    return high, (x - high.astype(F32)).astype(BF16)


def lane_sums(x):
    total = jnp.sum(x, axis=0, keepdims=True)
    out = total[:, 0:128]
    for k in range(1, x.shape[1] // 128):
        out = out + total[:, k * 128 : (k + 1) * 128]
    return out


def exchange_kernel(
    n, scale, blocks, dirn_hbm, pairs, band_hbm, offs_hbm,
    st_o, codes_o, v_o, f_o, z_o, norm_o,
    dirn, band, offs, in_sem, send_sem, recv_sem,
):
    me = lax.axis_index("tile")
    rows = pairs.shape[0]
    part = dirn.shape[1] // CHUNKS
    fetch_offs = pltpu.make_async_copy(offs_hbm, offs, in_sem.at[0])
    fetch_pairs = pltpu.make_async_copy(pairs, codes_o.at[REACH], in_sem.at[1])
    fetch_band = pltpu.make_async_copy(band_hbm, band, in_sem.at[2])
    fetch_dirn = [
        pltpu.make_async_copy(
            dirn_hbm.at[:, k * part : (k + 1) * part],
            dirn.at[:, k * part : (k + 1) * part],
            in_sem.at[3 + k],
        )
        for k in range(CHUNKS)
    ]
    for one in [fetch_offs, fetch_pairs, fetch_band] + fetch_dirn:
        one.start()
    barrier = pltpu.get_barrier_semaphore()
    for r in HOPS:
        @pl.when(exists(me, r, n))
        def _():
            pl.semaphore_signal(barrier, inc=1, device_id={"tile": me + r}, device_id_type=MESH)

    own = REACH * rows
    for r in HOPS:
        @pl.when(jnp.logical_not(exists(me, r, n)))
        def _():
            t = r + REACH
            st_o[t * rows : (t + 1) * rows] = jnp.zeros((rows,) + st_o.shape[1:], F32)
            codes_o[t] = jnp.full(codes_o.shape[1:], -1, jnp.int32)
    fetch_offs.wait()
    for k in range(rows):
        st_o[own + k] = offs[:, k * SBLOCK : (k + 1) * SBLOCK]
    fetch_pairs.wait()

    peers = sum(exists(me, r, n).astype(jnp.int32) for r in HOPS)
    pl.semaphore_wait(barrier, peers)

    def copies(q, r):
        t = REACH - r
        made = []
        for which, (src, dst) in enumerate((
            (codes_o.at[REACH], codes_o.at[t]),
            (st_o.at[pl.ds(own, rows)], st_o.at[pl.ds(t * rows, rows)]),
        )):
            made.append(pltpu.make_async_remote_copy(
                src_ref=src, dst_ref=dst, send_sem=send_sem.at[which, q],
                recv_sem=recv_sem.at[which, q], device_id={"tile": me + r}, device_id_type=MESH,
            ))
        return made

    for q, r in enumerate(HOPS):
        @pl.when(exists(me, r, n))
        def _():
            for one in copies(q, r):
                one.start()

    fetch_band.wait()
    depth = (band[...].astype(F32) + 0.5) * (DEPTH_RANGE / BANDS)
    shifted = depth + DEPTH_SHIFT
    f_o[...] = scale * depth * (shifted * jnp.sqrt(shifted))
    z_o[...] = (depth * depth).T

    def block(b, total):
        for q in range(CBLOCK // 128):
            lanes = pl.ds(pl.multiple_of(b * CBLOCK + q * 128, 128), 128)
            values = dirn[:, lanes]
            high, low = split(f_o[pl.ds(b * (CBLOCK // 128) + q, 1), :] * values)
            v_o[b, 0:16, q * 128 : (q + 1) * 128] = high
            v_o[b, 16:32, q * 128 : (q + 1) * 128] = low
            total = total + values * values
        return total

    total = jnp.zeros((dirn.shape[0], 128), F32)
    for k in range(CHUNKS):
        fetch_dirn[k].wait()
        total = lax.fori_loop(k * blocks // CHUNKS, (k + 1) * blocks // CHUNKS, block, total)
    norm_o[...] = jnp.broadcast_to(lane_sums(total), norm_o.shape)

    for q, r in enumerate(HOPS):
        @pl.when(exists(me, r, n))
        def _():
            for one in copies(q, r):
                one.wait_send()

        @pl.when(exists(me, -r, n))
        def _():
            for one in copies(q, r):
                one.wait_recv()


def kernel_halves(entry, st, z):
    j = lax.shift_right_logical(entry, 5)
    b = lax.bitwise_and(entry, 31)
    at = jnp.minimum(j, st.shape[0] - 1)
    rows = st.shape[0] // SPAN
    moved = (at // rows - REACH).astype(F32)
    parity = lax.bitwise_and(b, 1).astype(F32)
    place = st[at]
    sx = jnp.broadcast_to(place[0:1, :] + moved, (8, SBLOCK))
    sy = jnp.broadcast_to(place[1:2, :] - 0.5 * parity, (8, SBLOCK))
    column = (lax.broadcasted_iota(jnp.int32, (COL_SIDE, SBLOCK), 0).astype(F32) + 0.5) / COL_SIDE
    across = jnp.concatenate([sx] * (COL_SIDE // 8), axis=0) - column
    across = across * across
    which = jnp.full((COL_SIDE, 128), b * (CBLOCK // 128), jnp.int32)
    halves = []
    for h in range(2):
        highs, lows = [], []
        for a in range(h * 8, h * 8 + 8):
            along = sy - (a + 0.5) / COL_SIDE
            along = jnp.concatenate([along * along] * (COL_SIDE // 8), axis=0)
            low_row = a % 4 * COL_SIDE
            picked = jnp.take_along_axis(z[low_row : low_row + COL_SIDE, :], which + a // 4, axis=1)
            picked = jnp.concatenate([picked, picked], axis=1)
            inverse = lax.rsqrt(across + (along + picked))
            high, low = split(inverse * inverse * inverse)
            highs.append(high)
            lows.append(low)
        halves.append((jnp.concatenate(highs, axis=0), jnp.concatenate(lows, axis=0)))
    return j, b, halves


def forward_kernel(codes, st, z, v, img, pair_list, count):
    rows = codes.shape[1]
    img[...] = jnp.zeros(img.shape, F32)
    filled = jnp.int32(0)
    for t in range(SPAN):
        def pick(row, filled):
            for p in range(codes.shape[2]):
                code = codes[t, row, p]
                pair_list[filled] = (t * rows + row) * 32 + lax.bitwise_and(code, 31)
                hit = lax.shift_right_arithmetic(code, 5) == SPAN - 1 - t
                filled = filled + hit.astype(jnp.int32)
            return filled
        filled = lax.fori_loop(0, rows, pick, filled)
    for u in range(UNROLL):
        pair_list[filled + u] = SPAN * rows * 32
    steps = (filled + (UNROLL - 1)) // UNROLL
    count[0] = steps

    def step(i, carry):
        for u in range(UNROLL):
            j, b, halves = kernel_halves(pair_list[i * UNROLL + u], st, z)
            out = jnp.zeros((32, SBLOCK), F32)
            for h in range(2):
                values = v[b, :, h * 256 : (h + 1) * 256]
                for part in halves[h]:
                    out = out + jnp.dot(values, part, preferred_element_type=F32)
            img[j] += out[0:16] + out[16:32]
        return carry

    lax.fori_loop(0, steps, step, 0)


def all_sum(n, me, mine, landing, send_sem, recv_sem, start, finish):
    def made(k):
        return pltpu.make_async_remote_copy(
            src_ref=mine, dst_ref=landing.at[k], send_sem=send_sem.at[k], recv_sem=recv_sem.at[k],
            device_id={"tile": lax.rem(me + k, n)}, device_id_type=MESH,
        )
    if start:
        def go(k, c):
            made(k).start()
            return c
        lax.fori_loop(1, n, go, 0)
    if finish:
        def done(k, c):
            made(k).wait()
            return c
        lax.fori_loop(1, n, done, 0)


def greet(n, me):
    barrier = pltpu.get_barrier_semaphore()

    def one(k, c):
        pl.semaphore_signal(
            barrier, inc=1, device_id={"tile": lax.rem(me + k, n)}, device_id_type=MESH
        )
        return c
    lax.fori_loop(1, n, one, 0)


def greeted(n):
    pl.semaphore_wait(pltpu.get_barrier_semaphore(), n - 1)


def image_kernel(
    n, rows, img, res, norm, old, newres_o, scal_o,
    transit, joined, part_rx, norm_tx, norm_rx, send_sem, recv_sem, nsend_sem, nrecv_sem,
):
    me = lax.axis_index("tile")
    greet(n, me)
    greeted(n)
    s = 1 - 2 * lax.rem(me, 2)
    outward = exists(me, -2 * s, n)
    inward = exists(me, 2 * s, n)

    def slab(ref, r):
        return ref.at[pl.ds((REACH + r) * rows, rows)]

    def copy(number, src, dst, to):
        return pltpu.make_async_remote_copy(
            src_ref=src, dst_ref=dst, send_sem=send_sem.at[number],
            recv_sem=recv_sem.at[number], device_id={"tile": to}, device_id_type=MESH,
        )

    to_join = copy(0, slab(img, 2 * s), transit, me + s)
    to_sibling = copy(1, slab(img, s), part_rx.at[0], me + s)
    to_far = copy(2, slab(img, -2 * s), part_rx.at[1], me - 2 * s)
    to_near = copy(3, joined, part_rx.at[2], me - s)
    own = slab(newres_o, 0)
    give_near = copy(4, own, slab(newres_o, s), me - s)
    give_far = copy(5, own, slab(newres_o, -2 * s), me + 2 * s)
    give_sibling = copy(6, own, slab(newres_o, -s), me + s)
    pass_on = copy(7, slab(newres_o, -s), slab(newres_o, -2 * s), me + s)

    @pl.when(inward)
    def _():
        to_join.start()

    @pl.when(outward)
    def _():
        to_far.start()
    to_sibling.start()

    def squares(k, total):
        values = old[:, pl.ds(pl.multiple_of(k * 512, 512), 512)]
        return total + values * values

    before = lax.fori_loop(0, old.shape[1] // 512, squares, jnp.zeros((old.shape[0], 512), F32))
    lane = lax.broadcasted_iota(jnp.int32, (1, 128), 1)
    gamma_part = jnp.sum(lane_sums(before), axis=1, keepdims=True)
    norm_part = DAMPING * jnp.sum(norm[0:1, :], axis=1, keepdims=True)
    known = jnp.where(lane == 0, gamma_part, jnp.where(lane == 1, norm_part, 0.0))

    @pl.when(outward)
    def _():
        to_join.wait_recv()
        joined[...] = transit[...] + img[pl.ds((REACH - s) * rows, rows)]
        to_near.start()

    to_sibling.wait_recv()
    here = REACH * rows
    newres_o[here : here + rows] = img[here : here + rows] + part_rx[0]

    @pl.when(inward)
    def _():
        to_far.wait_recv()
        newres_o[here : here + rows] += part_rx[1]

    @pl.when(outward)
    def _():
        to_near.wait_recv()
        newres_o[here : here + rows] += part_rx[2]

    image = newres_o[here : here + rows]
    squared = lane_sums(jnp.sum(image * image, axis=0))
    folded = squared + jnp.where(lane == 1, 0.0, pltpu.roll(jnp.where(lane < 2, squared, 0.0), 2, 1))
    norm_tx[...] = jnp.where(lane < 2, known, folded)
    all_sum(n, me, norm_tx, norm_rx, nsend_sem, nrecv_sem, True, True)
    norm_rx[0] = norm_tx[...]
    totals = jnp.sum(norm_rx[...], axis=0)
    gamma_old = jnp.sum(jnp.where(lane == 0, totals, 0.0), axis=1, keepdims=True)
    curvature = jnp.sum(jnp.where(lane == 0, 0.0, totals), axis=1, keepdims=True)
    length = gamma_old / (curvature + GUARD)
    scal_o[...] = jnp.concatenate(
        [jnp.broadcast_to(length, (4, 128)), jnp.broadcast_to(gamma_old, (4, 128))], axis=0
    )
    for k in range(rows):
        newres_o[here + k] = res[:, k * SBLOCK : (k + 1) * SBLOCK] - length * newres_o[here + k]

    @pl.when(outward)
    def _():
        give_near.start()

    @pl.when(inward)
    def _():
        give_far.start()
    give_sibling.start()

    @pl.when(outward)
    def _():
        give_near.wait_recv()
        pass_on.start()
        to_far.wait_send()
        to_near.wait_send()
        give_far.wait_recv()
        give_near.wait_send()
        pass_on.wait_send()

    @pl.when(inward)
    def _():
        to_join.wait_send()
        give_far.wait_send()
        pass_on.wait_recv()
    to_sibling.wait_send()
    give_sibling.wait()


def adjoint_kernel(
    pair_list, count, st, z, newres, scal, model, dirn,
    model_hbm, model_o, acc, res_o, parts, out_sem,
):
    slots = newres.shape[0]
    rows = slots // SPAN
    for k in range(rows):
        res_o[:, k * SBLOCK : (k + 1) * SBLOCK] = newres[REACH * rows + k]

    length = scal[0:1, 0:1]

    def update(b, c):
        lanes = pl.ds(pl.multiple_of(b * CBLOCK, CBLOCK), CBLOCK)
        model_o[:, lanes] = model[:, lanes] + length * dirn[:, lanes]
        return c
    lax.fori_loop(0, acc.shape[0], update, 0)
    leave = pltpu.make_async_copy(model_o, model_hbm, out_sem)
    leave.start()

    def cut(k, c):
        high, low = split(newres[k])
        parts[k, 0:16, :] = high
        parts[k, 16:32, :] = low
        return c
    lax.fori_loop(0, slots, cut, 0)
    parts[slots] = jnp.zeros((32, SBLOCK), BF16)
    acc[...] = jnp.zeros(acc.shape, F32)

    def step(i, carry):
        for u in range(UNROLL):
            j, b, halves = kernel_halves(pair_list[i * UNROLL + u], st, z)
            values = parts[j]
            for h in range(2):
                out = jnp.zeros((32, 256), F32)
                for part in halves[h]:
                    out = out + lax.dot_general(
                        values, part, (((1,), (1,)), ((), ())), preferred_element_type=F32
                    )
                acc[b, :, h * 256 : (h + 1) * 256] += out[0:16] + out[16:32]
        return carry

    lax.fori_loop(0, count[0], step, 0)

    leave.wait()


def gamma_kernel(n, acc, model, f, scal, grad_o, ratio_o, mine, landing, send_sem, recv_sem):
    me = lax.axis_index("tile")
    greet(n, me)

    def finish(b, total):
        lanes = pl.ds(pl.multiple_of(b * CBLOCK, CBLOCK), CBLOCK)
        factor = jnp.concatenate(
            [f[pl.ds(b * (CBLOCK // 128) + q, 1), :] for q in range(CBLOCK // 128)], axis=1
        )
        gradient = factor * acc[b] - DAMPING * model[:, lanes]
        grad_o[:, lanes] = gradient
        return total + gradient * gradient

    total = lax.fori_loop(0, acc.shape[0], finish, jnp.zeros((model.shape[0], CBLOCK), F32))
    mine[...] = lane_sums(total)
    greeted(n)
    all_sum(n, me, mine, landing, send_sem, recv_sem, True, True)
    landing[0] = mine[...]
    total = jnp.sum(jnp.sum(landing[...], axis=0), axis=1, keepdims=True)
    ratio_o[...] = total / (scal[4:5, 0:1] + GUARD)


def shards(model_field, direction, old_grad, residual, block_pairs, depth_band, station_offsets):
    n = lax.axis_size("tile")
    epochs, cells = model_field.shape
    stations = residual.shape[1]
    rows = block_pairs.shape[0]
    pairs = block_pairs.shape[1]
    blocks = cells // CBLOCK
    scale = 2.0 / math.sqrt(cells)
    vmem = pl.BlockSpec(memory_space=pltpu.VMEM)
    smem = pl.BlockSpec(memory_space=pltpu.SMEM)
    hbm = pl.BlockSpec(memory_space=pltpu.HBM)
    shape = jax.ShapeDtypeStruct
    slots = SPAN * rows
    dma = pltpu.SemaphoreType.DMA

    def params(number=None):
        if number is None:
            return pltpu.CompilerParams(vmem_limit_bytes=VMEM_LIMIT)
        return pltpu.CompilerParams(
            vmem_limit_bytes=VMEM_LIMIT, collective_id=number, has_side_effects=True
        )

    st, codes, v, f, z, norm = pl.pallas_call(
        functools.partial(exchange_kernel, n, scale, blocks),
        out_shape=(
            shape((slots, 2, SBLOCK), F32),
            shape((SPAN, rows, pairs), jnp.int32),
            shape((blocks, 2 * epochs, CBLOCK), BF16),
            shape((cells // 128, 128), F32),
            shape((128, cells // 128), F32),
            shape((8, 128), F32),
        ),
        in_specs=[hbm] * 4,
        out_specs=(vmem,) * 6,
        scratch_shapes=[
            pltpu.VMEM((epochs, cells), F32),
            pltpu.VMEM((cells // 128, 128), jnp.int32),
            pltpu.VMEM((2, stations), F32),
            dma((3 + CHUNKS,)),
            dma((2, len(HOPS))),
            dma((2, len(HOPS))),
        ],
        compiler_params=params(0),
        name="exchange",
    )(*(
        pltpu.with_memory_space_constraint(one, pltpu.HBM)
        for one in (direction, block_pairs, depth_band.reshape(cells // 128, 128), station_offsets)
    ))

    img, pair_list, count = pl.pallas_call(
        forward_kernel,
        out_shape=(
            shape((slots + 1, epochs, SBLOCK), F32),
            shape((slots * pairs + UNROLL,), jnp.int32),
            shape((1,), jnp.int32),
        ),
        in_specs=[smem, vmem, vmem, vmem],
        out_specs=(vmem, smem, smem),
        compiler_params=params(),
        name="forward",
    )(codes, st, z, v)

    newres, scal = pl.pallas_call(
        functools.partial(image_kernel, n, rows),
        out_shape=(shape((slots, epochs, SBLOCK), F32), shape((8, 128), F32)),
        in_specs=[vmem] * 4,
        out_specs=(vmem,) * 2,
        scratch_shapes=[
            pltpu.VMEM((rows, epochs, SBLOCK), F32),
            pltpu.VMEM((rows, epochs, SBLOCK), F32),
            pltpu.VMEM((3, rows, epochs, SBLOCK), F32),
            pltpu.VMEM((1, 128), F32),
            pltpu.VMEM((n, 1, 128), F32),
            dma((8,)),
            dma((8,)),
            dma((n,)),
            dma((n,)),
        ],
        compiler_params=params(1),
        name="images",
    )(img, residual, norm, old_grad)

    new_model, model_kept, acc, new_residual = pl.pallas_call(
        adjoint_kernel,
        out_shape=(
            shape((epochs, cells), F32),
            shape((epochs, cells), F32),
            shape((blocks, epochs, CBLOCK), F32),
            shape((epochs, stations), F32),
        ),
        in_specs=[smem, smem] + [vmem] * 6,
        out_specs=(hbm,) + (vmem,) * 3,
        scratch_shapes=[pltpu.VMEM((slots + 1, 2 * epochs, SBLOCK), BF16), dma(())],
        compiler_params=params(),
        name="adjoint",
    )(pair_list, count, st, z, newres, scal, model_field, direction)

    gradient, ratio = pl.pallas_call(
        functools.partial(gamma_kernel, n),
        out_shape=(shape((epochs, cells), F32), shape((1, 1), F32)),
        in_specs=[vmem] * 4,
        out_specs=(vmem,) * 2,
        scratch_shapes=[
            pltpu.VMEM((1, 128), F32), pltpu.VMEM((n, 1, 128), F32), dma((n,)), dma((n,)),
        ],
        compiler_params=params(2),
        name="gamma",
    )(acc, model_kept, f, scal)
    new_direction = gradient + ratio.reshape(()) * direction
    return (new_model, new_residual, new_direction)


def solution(mesh):
    both = ("groups", "tile")
    wide = P(None, both)
    return jax.shard_map(
        shards,
        mesh=mesh,
        in_specs=(wide, wide, wide, wide, P(both, None), P(both), wide),
        out_specs=(wide, wide, wide),
        check_vma=False,
    )
```

```python
import functools
import math

import jax
import jax.numpy as jnp
from jax import lax
from jax.experimental import pallas as pl
from jax.experimental.pallas import tpu as pltpu
from jax.sharding import PartitionSpec as P

CBLOCK = 512
SBLOCK = 256
REACH = 2
BANDS = 16
COL_SIDE = 32
DEPTH_RANGE = 2.0
DEPTH_SHIFT = 0.25
DAMPING = 1.0
GUARD = 1e-06

SPAN = 2 * REACH + 1
CHUNKS = 4
HOPS = tuple(r for r in range(-REACH, REACH + 1) if r != 0)
UNROLL = 8
KEPT = 88
STRIP = 64
STRETCH = 4.0
MESH = pl.DeviceIdType.MESH
F32 = jnp.float32
BF16 = jnp.bfloat16
VMEM_LIMIT = 4 * 1024 * 1024


def exists(me, r, n):
    return jnp.logical_and(me + r >= 0, me + r < n)


def split(x):
    high = x.astype(BF16)
    return high, (x - high.astype(F32)).astype(BF16)


def lane_sums(x):
    total = jnp.sum(x, axis=0, keepdims=True)
    out = total[:, 0:128]
    for k in range(1, x.shape[1] // 128):
        out = out + total[:, k * 128 : (k + 1) * 128]
    return out


def exchange_kernel(
    n, scale, blocks, dirn_hbm, pairs, band_hbm, offs_hbm,
    st_o, codes_o, v_o, f_o, z_o, norm_o,
    dirn, band, offs, in_sem, send_sem, recv_sem,
):
    me = lax.axis_index("tile")
    rows = pairs.shape[0]
    part = dirn.shape[1] // CHUNKS
    fetch_offs = pltpu.make_async_copy(offs_hbm, offs, in_sem.at[0])
    fetch_pairs = pltpu.make_async_copy(pairs, codes_o.at[REACH], in_sem.at[1])
    fetch_band = pltpu.make_async_copy(band_hbm, band, in_sem.at[2])
    fetch_dirn = [
        pltpu.make_async_copy(
            dirn_hbm.at[:, k * part : (k + 1) * part],
            dirn.at[:, k * part : (k + 1) * part],
            in_sem.at[3 + k],
        )
        for k in range(CHUNKS)
    ]
    for one in [fetch_offs, fetch_pairs, fetch_band] + fetch_dirn:
        one.start()
    barrier = pltpu.get_barrier_semaphore()
    for r in HOPS:
        @pl.when(exists(me, r, n))
        def _():
            pl.semaphore_signal(barrier, inc=1, device_id={"tile": me + r}, device_id_type=MESH)

    own = REACH * rows
    for r in HOPS:
        @pl.when(jnp.logical_not(exists(me, r, n)))
        def _():
            t = r + REACH
            st_o[:, t * rows : (t + 1) * rows] = jnp.zeros((2, rows, SBLOCK), F32)
            codes_o[t] = jnp.full(codes_o.shape[1:], -1, jnp.int32)
    fetch_offs.wait()
    for k in range(rows):
        for w in range(2):
            st_o[w, own + k : own + k + 1] = offs[w : w + 1, k * SBLOCK : (k + 1) * SBLOCK]
    fetch_pairs.wait()

    peers = sum(exists(me, r, n).astype(jnp.int32) for r in HOPS)
    pl.semaphore_wait(barrier, peers)

    def copies(q, r):
        t = REACH - r
        made = []
        for which, (src, dst) in enumerate((
            (codes_o.at[REACH], codes_o.at[t]),
            (st_o.at[:, pl.ds(own, rows)], st_o.at[:, pl.ds(t * rows, rows)]),
        )):
            made.append(pltpu.make_async_remote_copy(
                src_ref=src, dst_ref=dst, send_sem=send_sem.at[which, q],
                recv_sem=recv_sem.at[which, q], device_id={"tile": me + r}, device_id_type=MESH,
            ))
        return made

    for q, r in enumerate(HOPS):
        @pl.when(exists(me, r, n))
        def _():
            for one in copies(q, r):
                one.start()

    fetch_band.wait()
    depth = (band[...].astype(F32) + 0.5) * (DEPTH_RANGE / BANDS)
    shifted = depth + DEPTH_SHIFT
    f_o[...] = (scale * STRETCH**3) * depth * (shifted * jnp.sqrt(shifted))
    q = lax.bitwise_and(lax.broadcasted_iota(jnp.int32, z_o.shape, 0), 3).astype(F32)
    z_o[...] = (STRETCH * STRETCH) * (depth * depth) + 0.25 * (q * q)

    def block(b, total):
        for q in range(CBLOCK // 128):
            lanes = pl.ds(pl.multiple_of(b * CBLOCK + q * 128, 128), 128)
            values = dirn[:, lanes]
            high, low = split(f_o[pl.ds(b * (CBLOCK // 128) + q, 1), :] * values)
            v_o[b, 0:16, q * 128 : (q + 1) * 128] = high
            v_o[b, 16:32, q * 128 : (q + 1) * 128] = low
            total = total + values * values
        return total

    total = jnp.zeros((dirn.shape[0], 128), F32)
    for k in range(CHUNKS):
        fetch_dirn[k].wait()
        total = lax.fori_loop(k * blocks // CHUNKS, (k + 1) * blocks // CHUNKS, block, total)
    norm_o[...] = jnp.broadcast_to(lane_sums(total), norm_o.shape)

    for q, r in enumerate(HOPS):
        @pl.when(exists(me, r, n))
        def _():
            for one in copies(q, r):
                one.wait_send()

        @pl.when(exists(me, -r, n))
        def _():
            for one in copies(q, r):
                one.wait_recv()


def fill_block(entry, slots, places, z, dst):
    j = lax.shift_right_logical(entry, 5)
    b = lax.bitwise_and(entry, 31)
    at = jnp.minimum(j, slots - 1)
    parity = lax.bitwise_and(b, 1).astype(F32)
    lane = lax.broadcasted_iota(jnp.int32, (8, 128), 1)
    unit = STRETCH / COL_SIDE
    cell_across = (lax.rem(lane, COL_SIDE).astype(F32) + 0.5) * unit
    cell_along = (lax.div(lane, COL_SIDE).astype(F32) + 0.5) * unit + (0.5 * STRETCH) * parity
    cell_across = jnp.concatenate([cell_across] * (STRIP // 8), axis=0)
    cell_along = jnp.concatenate([cell_along] * (STRIP // 8), axis=0)
    which = jnp.full((STRIP, 128), at, jnp.int32)
    deeps = [
        jnp.broadcast_to(z[pl.ds(b * (CBLOCK // 128) + q, 1), :], (8, 128))
        for q in range(CBLOCK // 128)
    ]
    for k in range(SBLOCK // STRIP):
        rows = slice(k * STRIP, (k + 1) * STRIP)
        across = jnp.take_along_axis(places[0, rows, :], which, axis=1) - cell_across
        along = jnp.take_along_axis(places[1, rows, :], which, axis=1) - cell_along
        flat = across * across + along * along
        for q in range(CBLOCK // 128):
            if q > 0:
                flat = flat - along
            inverse = lax.rsqrt(flat + jnp.concatenate([deeps[q]] * (STRIP // 8), axis=0))
            high, low = split(inverse * inverse * inverse)
            dst[0, q, rows, :] = high
            dst[1, q, rows, :] = low
    return j, b


def block_part(block, w):
    return jnp.concatenate([block[w, q] for q in range(CBLOCK // 128)], axis=1)


def forward_kernel(codes, st, z, v, img, pair_list, count, places, *rest):
    kept, spare = rest[:UNROLL], rest[UNROLL]
    slots = st.shape[1]
    pad = jnp.zeros((128 - slots, SBLOCK), F32)
    shift = lax.broadcasted_iota(jnp.int32, (slots, SBLOCK), 0) // codes.shape[1] - REACH
    places[0] = jnp.concatenate([STRETCH * (st[0] + shift.astype(F32)), pad], axis=0).T
    places[1] = jnp.concatenate([STRETCH * st[1], pad], axis=0).T
    rows = codes.shape[1]
    img[...] = jnp.zeros(img.shape, F32)
    filled = jnp.int32(0)
    for t in range(SPAN):
        def pick(row, filled):
            for p in range(codes.shape[2]):
                code = codes[t, row, p]
                pair_list[filled] = (t * rows + row) * 32 + lax.bitwise_and(code, 31)
                hit = lax.shift_right_arithmetic(code, 5) == SPAN - 1 - t
                filled = filled + hit.astype(jnp.int32)
            return filled
        filled = lax.fori_loop(0, rows, pick, filled)
    for u in range(UNROLL):
        pair_list[filled + u] = SPAN * rows * 32
    steps = (filled + (UNROLL - 1)) // UNROLL
    count[0] = steps
    count[1] = jnp.minimum(steps, KEPT // UNROLL)

    def step(keep, i, carry):
        for u in range(UNROLL):
            block = kept[u].at[i] if keep else spare
            j, b = fill_block(pair_list[i * UNROLL + u], slots, places, z, block)
            out = jnp.zeros((32, SBLOCK), F32)
            for w in range(2):
                out = out + lax.dot_general(
                    v[b], block_part(block, w), (((1,), (1,)), ((), ())), preferred_element_type=F32
                )
            img[j] += out[0:16] + out[16:32]
        return carry

    lax.fori_loop(0, count[1], functools.partial(step, True), 0)
    lax.fori_loop(count[1], steps, functools.partial(step, False), 0)


def all_sum(n, me, mine, landing, send_sem, recv_sem, start, finish):
    def made(k):
        return pltpu.make_async_remote_copy(
            src_ref=mine, dst_ref=landing.at[k], send_sem=send_sem.at[k], recv_sem=recv_sem.at[k],
            device_id={"tile": lax.rem(me + k, n)}, device_id_type=MESH,
        )
    if start:
        def go(k, c):
            made(k).start()
            return c
        lax.fori_loop(1, n, go, 0)
    if finish:
        def done(k, c):
            made(k).wait()
            return c
        lax.fori_loop(1, n, done, 0)


def greet(n, me):
    barrier = pltpu.get_barrier_semaphore()

    def one(k, c):
        pl.semaphore_signal(
            barrier, inc=1, device_id={"tile": lax.rem(me + k, n)}, device_id_type=MESH
        )
        return c
    lax.fori_loop(1, n, one, 0)


def greeted(n):
    pl.semaphore_wait(pltpu.get_barrier_semaphore(), n - 1)


def image_kernel(
    n, rows, img, res_hbm, norm, old_hbm, newres_o, scal_o,
    res, old, in_sem, transit, joined, part_rx, norm_tx, norm_rx, send_sem, recv_sem, nsend_sem, nrecv_sem,
):
    me = lax.axis_index("tile")
    greet(n, me)
    fetch_old = pltpu.make_async_copy(old_hbm, old, in_sem.at[0])
    fetch_res = pltpu.make_async_copy(res_hbm, res, in_sem.at[1])
    fetch_old.start()
    fetch_res.start()
    greeted(n)
    s = 1 - 2 * lax.rem(me, 2)
    outward = exists(me, -2 * s, n)
    inward = exists(me, 2 * s, n)

    def slab(ref, r):
        return ref.at[pl.ds((REACH + r) * rows, rows)]

    def copy(number, src, dst, to):
        return pltpu.make_async_remote_copy(
            src_ref=src, dst_ref=dst, send_sem=send_sem.at[number],
            recv_sem=recv_sem.at[number], device_id={"tile": to}, device_id_type=MESH,
        )

    to_join = copy(0, slab(img, 2 * s), transit, me + s)
    to_sibling = copy(1, slab(img, s), part_rx.at[0], me + s)
    to_far = copy(2, slab(img, -2 * s), part_rx.at[1], me - 2 * s)
    to_near = copy(3, joined, part_rx.at[2], me - s)
    own = slab(newres_o, 0)
    give_near = copy(4, own, slab(newres_o, s), me - s)
    give_far = copy(5, own, slab(newres_o, -2 * s), me + 2 * s)
    give_sibling = copy(6, own, slab(newres_o, -s), me + s)
    pass_on = copy(7, slab(newres_o, -s), slab(newres_o, -2 * s), me + s)

    @pl.when(inward)
    def _():
        to_join.start()

    @pl.when(outward)
    def _():
        to_far.start()
    to_sibling.start()

    def squares(k, total):
        values = old[:, pl.ds(pl.multiple_of(k * 512, 512), 512)]
        return total + values * values

    fetch_old.wait()
    fetch_res.wait()
    before = lax.fori_loop(0, old.shape[1] // 512, squares, jnp.zeros((old.shape[0], 512), F32))
    lane = lax.broadcasted_iota(jnp.int32, (1, 128), 1)
    gamma_part = jnp.sum(lane_sums(before), axis=1, keepdims=True)
    norm_part = DAMPING * jnp.sum(norm[0:1, :], axis=1, keepdims=True)
    known = jnp.where(lane == 0, gamma_part, jnp.where(lane == 1, norm_part, 0.0))

    @pl.when(outward)
    def _():
        to_join.wait_recv()
        joined[...] = transit[...] + img[pl.ds((REACH - s) * rows, rows)]
        to_near.start()

    to_sibling.wait_recv()
    here = REACH * rows
    newres_o[here : here + rows] = img[here : here + rows] + part_rx[0]

    @pl.when(inward)
    def _():
        to_far.wait_recv()
        newres_o[here : here + rows] += part_rx[1]

    @pl.when(outward)
    def _():
        to_near.wait_recv()
        newres_o[here : here + rows] += part_rx[2]

    image = newres_o[here : here + rows]
    squared = lane_sums(jnp.sum(image * image, axis=0))
    folded = squared + jnp.where(lane == 1, 0.0, pltpu.roll(jnp.where(lane < 2, squared, 0.0), 2, 1))
    norm_tx[...] = jnp.where(lane < 2, known, folded)
    all_sum(n, me, norm_tx, norm_rx, nsend_sem, nrecv_sem, True, True)
    norm_rx[0] = norm_tx[...]
    totals = jnp.sum(norm_rx[...], axis=0)
    gamma_old = jnp.sum(jnp.where(lane == 0, totals, 0.0), axis=1, keepdims=True)
    curvature = jnp.sum(jnp.where(lane == 0, 0.0, totals), axis=1, keepdims=True)
    length = gamma_old / (curvature + GUARD)
    scal_o[...] = jnp.concatenate(
        [jnp.broadcast_to(length, (4, 128)), jnp.broadcast_to(gamma_old, (4, 128))], axis=0
    )
    for k in range(rows):
        newres_o[here + k] = res[:, k * SBLOCK : (k + 1) * SBLOCK] - length * newres_o[here + k]

    @pl.when(outward)
    def _():
        give_near.start()

    @pl.when(inward)
    def _():
        give_far.start()
    give_sibling.start()

    @pl.when(outward)
    def _():
        give_near.wait_recv()
        pass_on.start()
        to_far.wait_send()
        to_near.wait_send()
        give_far.wait_recv()
        give_near.wait_send()
        pass_on.wait_send()

    @pl.when(inward)
    def _():
        to_join.wait_send()
        give_far.wait_send()
        pass_on.wait_recv()
    to_sibling.wait_send()
    give_sibling.wait()


def adjoint_kernel(pair_list, count, places, z, newres, scal, model_in, dirn_in, *rest):
    kept = rest[:UNROLL]
    model_hbm, model_o, acc, res_o, dirn, parts, spare, in_sem, out_sem = rest[UNROLL:]
    slots = newres.shape[0]
    rows = slots // SPAN
    fetch_model = pltpu.make_async_copy(model_in, model_o, in_sem.at[0])
    fetch_dirn = pltpu.make_async_copy(dirn_in, dirn, in_sem.at[1])
    fetch_model.start()
    fetch_dirn.start()
    for k in range(rows):
        res_o[:, k * SBLOCK : (k + 1) * SBLOCK] = newres[REACH * rows + k]

    def cut(k, c):
        high, low = split(newres[k])
        parts[k, 0:16, :] = high
        parts[k, 16:32, :] = low
        return c
    lax.fori_loop(0, slots, cut, 0)
    parts[slots] = jnp.zeros((32, SBLOCK), BF16)
    acc[...] = jnp.zeros(acc.shape, F32)

    def add_pair(j, b, block):
        out = jnp.zeros((32, CBLOCK), F32)
        for w in range(2):
            out = out + jnp.dot(parts[j], block_part(block, w), preferred_element_type=F32)
        acc[b] += out[0:16] + out[16:32]

    def reread(i, carry):
        for u in range(UNROLL):
            entry = pair_list[i * UNROLL + u]
            add_pair(lax.shift_right_logical(entry, 5), lax.bitwise_and(entry, 31), kept[u].at[i])
        return carry

    def rebuild(i, carry):
        for u in range(UNROLL):
            j, b = fill_block(pair_list[i * UNROLL + u], slots, places, z, spare)
            add_pair(j, b, spare)
        return carry

    first = jnp.minimum(count[1], 1)
    lax.fori_loop(0, first, reread, 0)
    fetch_model.wait()
    fetch_dirn.wait()
    length = scal[0:1, 0:1]

    def update(b, c):
        lanes = pl.ds(pl.multiple_of(b * CBLOCK, CBLOCK), CBLOCK)
        model_o[:, lanes] = model_o[:, lanes] + length * dirn[:, lanes]
        return c
    lax.fori_loop(0, acc.shape[0], update, 0)
    leave = pltpu.make_async_copy(model_o, model_hbm, out_sem)
    leave.start()
    lax.fori_loop(first, count[1], reread, 0)
    lax.fori_loop(count[1], count[0], rebuild, 0)
    leave.wait()


def gamma_kernel(n, acc, model, f, scal, grad_o, ratio_o, mine, landing, send_sem, recv_sem):
    me = lax.axis_index("tile")
    greet(n, me)

    def finish(b, total):
        lanes = pl.ds(pl.multiple_of(b * CBLOCK, CBLOCK), CBLOCK)
        factor = jnp.concatenate(
            [f[pl.ds(b * (CBLOCK // 128) + q, 1), :] for q in range(CBLOCK // 128)], axis=1
        )
        gradient = factor * acc[b] - DAMPING * model[:, lanes]
        grad_o[:, lanes] = gradient
        return total + gradient * gradient

    total = lax.fori_loop(0, acc.shape[0], finish, jnp.zeros((model.shape[0], CBLOCK), F32))
    mine[...] = lane_sums(total)
    greeted(n)
    all_sum(n, me, mine, landing, send_sem, recv_sem, True, True)
    landing[0] = mine[...]
    total = jnp.sum(jnp.sum(landing[...], axis=0), axis=1, keepdims=True)
    ratio_o[...] = total / (scal[4:5, 0:1] + GUARD)


def shards(model_field, direction, old_grad, residual, block_pairs, depth_band, station_offsets):
    n = lax.axis_size("tile")
    epochs, cells = model_field.shape
    stations = residual.shape[1]
    rows = block_pairs.shape[0]
    pairs = block_pairs.shape[1]
    blocks = cells // CBLOCK
    scale = 2.0 / math.sqrt(cells)
    vmem = pl.BlockSpec(memory_space=pltpu.VMEM)
    smem = pl.BlockSpec(memory_space=pltpu.SMEM)
    hbm = pl.BlockSpec(memory_space=pltpu.HBM)
    shape = jax.ShapeDtypeStruct
    slots = SPAN * rows
    one_block = (2, CBLOCK // 128, SBLOCK, 128)
    dma = pltpu.SemaphoreType.DMA

    def in_hbm(one):
        return pltpu.with_memory_space_constraint(one, pltpu.HBM)

    def params(number=None):
        if number is None:
            return pltpu.CompilerParams(vmem_limit_bytes=VMEM_LIMIT)
        return pltpu.CompilerParams(
            vmem_limit_bytes=VMEM_LIMIT, collective_id=number, has_side_effects=True
        )

    st, codes, v, f, z, norm = pl.pallas_call(
        functools.partial(exchange_kernel, n, scale, blocks),
        out_shape=(
            shape((2, slots, SBLOCK), F32),
            shape((SPAN, rows, pairs), jnp.int32),
            shape((blocks, 2 * epochs, CBLOCK), BF16),
            shape((cells // 128, 128), F32),
            shape((cells // 128, 128), F32),
            shape((8, 128), F32),
        ),
        in_specs=[hbm] * 4,
        out_specs=(vmem,) * 6,
        scratch_shapes=[
            pltpu.VMEM((epochs, cells), F32),
            pltpu.VMEM((cells // 128, 128), jnp.int32),
            pltpu.VMEM((2, stations), F32),
            dma((3 + CHUNKS,)),
            dma((2, len(HOPS))),
            dma((2, len(HOPS))),
        ],
        compiler_params=params(0),
        name="exchange",
    )(
        in_hbm(direction), in_hbm(block_pairs),
        in_hbm(depth_band.reshape(cells // 128, 128)), in_hbm(station_offsets),
    )

    img, pair_list, count, places, *kept = pl.pallas_call(
        forward_kernel,
        out_shape=(
            shape((slots + 1, epochs, SBLOCK), F32),
            shape((slots * pairs + UNROLL,), jnp.int32),
            shape((2,), jnp.int32),
            shape((2, SBLOCK, 128), F32),
        ) + (pltpu.VMEM((KEPT // UNROLL,) + one_block, BF16),) * UNROLL,
        in_specs=[smem, vmem, vmem, vmem],
        out_specs=(vmem, smem, smem) + (vmem,) * (1 + UNROLL),
        scratch_shapes=[pltpu.VMEM(one_block, BF16)],
        compiler_params=params(),
        name="forward",
    )(codes, st, z, v)

    kept = [pltpu.with_memory_space_constraint(one, pltpu.VMEM) for one in kept]
    newres, scal = pl.pallas_call(
        functools.partial(image_kernel, n, rows),
        out_shape=(shape((slots, epochs, SBLOCK), F32), shape((8, 128), F32)),
        in_specs=[vmem, hbm, vmem, hbm],
        out_specs=(vmem,) * 2,
        scratch_shapes=[
            pltpu.VMEM((epochs, stations), F32),
            pltpu.VMEM((epochs, cells), F32),
            dma((2,)),
            pltpu.VMEM((rows, epochs, SBLOCK), F32),
            pltpu.VMEM((rows, epochs, SBLOCK), F32),
            pltpu.VMEM((3, rows, epochs, SBLOCK), F32),
            pltpu.VMEM((1, 128), F32),
            pltpu.VMEM((n, 1, 128), F32),
            dma((8,)),
            dma((8,)),
            dma((n,)),
            dma((n,)),
        ],
        compiler_params=params(1),
        name="images",
    )(img, in_hbm(residual), norm, in_hbm(old_grad))

    new_model, model_kept, acc, new_residual = pl.pallas_call(
        adjoint_kernel,
        out_shape=(
            shape((epochs, cells), F32),
            shape((epochs, cells), F32),
            shape((blocks, epochs, CBLOCK), F32),
            shape((epochs, stations), F32),
        ),
        in_specs=[smem, smem] + [vmem] * 4 + [hbm] * 2 + [vmem] * UNROLL,
        out_specs=(hbm,) + (vmem,) * 3,
        scratch_shapes=[
            pltpu.VMEM((epochs, cells), F32),
            pltpu.VMEM((slots + 1, 2 * epochs, SBLOCK), BF16),
            pltpu.VMEM(one_block, BF16),
            dma((2,)),
            dma(()),
        ],
        compiler_params=params(),
        name="adjoint",
    )(
        pair_list, count, places, z, newres, scal, in_hbm(model_field), in_hbm(direction), *kept
    )

    gradient, ratio = pl.pallas_call(
        functools.partial(gamma_kernel, n),
        out_shape=(shape((epochs, cells), F32), shape((1, 1), F32)),
        in_specs=[vmem] * 4,
        out_specs=(vmem,) * 2,
        scratch_shapes=[
            pltpu.VMEM((1, 128), F32), pltpu.VMEM((n, 1, 128), F32), dma((n,)), dma((n,)),
        ],
        compiler_params=params(2),
        name="gamma",
    )(acc, model_kept, f, scal)
    new_direction = gradient + ratio.reshape(()) * direction
    return (new_model, new_residual, new_direction)


def solution(mesh):
    both = ("groups", "tile")
    wide = P(None, both)
    return jax.shard_map(
        shards,
        mesh=mesh,
        in_specs=(wide, wide, wide, wide, P(both, None), P(both), wide),
        out_specs=(wide, wide, wide),
        check_vma=False,
    )
```

```python
import functools
import math

import jax
import jax.numpy as jnp
from jax import lax
from jax.experimental import pallas as pl
from jax.experimental.pallas import tpu as pltpu
from jax.sharding import PartitionSpec as P

CBLOCK = 512
SBLOCK = 256
REACH = 2
BANDS = 16
COL_SIDE = 32
DEPTH_RANGE = 2.0
DEPTH_SHIFT = 0.25
DAMPING = 1.0
GUARD = 1e-06

SPAN = 2 * REACH + 1
CHUNKS = 4
HOPS = tuple(r for r in range(-REACH, REACH + 1) if r != 0)
UNROLL = 8
KEPT = 88
STRIP = 64
STRETCH = 4.0
MESH = pl.DeviceIdType.MESH
F32 = jnp.float32
BF16 = jnp.bfloat16
VMEM_LIMIT = 4 * 1024 * 1024


def exists(me, r, n):
    return jnp.logical_and(me + r >= 0, me + r < n)


def split(x):
    high = x.astype(BF16)
    return high, (x - high.astype(F32)).astype(BF16)


def lane_sums(x):
    total = jnp.sum(x, axis=0, keepdims=True)
    out = total[:, 0:128]
    for k in range(1, x.shape[1] // 128):
        out = out + total[:, k * 128 : (k + 1) * 128]
    return out


def exchange_kernel(
    n, scale, blocks, dirn_hbm, pairs, band_hbm, offs_hbm,
    st_o, entries_o, v_o, f_o, z_o, norm_o, codes_o,
    dirn, band, offs, in_sem, send_sem, recv_sem,
):
    me = lax.axis_index("tile")
    rows = pairs.shape[0]
    part = dirn.shape[1] // CHUNKS
    fetch_offs = pltpu.make_async_copy(offs_hbm, offs, in_sem.at[0])
    fetch_pairs = pltpu.make_async_copy(pairs, codes_o.at[REACH], in_sem.at[1])
    fetch_band = pltpu.make_async_copy(band_hbm, band, in_sem.at[2])
    fetch_dirn = [
        pltpu.make_async_copy(
            dirn_hbm.at[:, k * part : (k + 1) * part],
            dirn.at[:, k * part : (k + 1) * part],
            in_sem.at[3 + k],
        )
        for k in range(CHUNKS)
    ]
    for one in [fetch_offs, fetch_pairs, fetch_band] + fetch_dirn:
        one.start()
    barrier = pltpu.get_barrier_semaphore()
    for r in HOPS:
        @pl.when(exists(me, r, n))
        def _():
            pl.semaphore_signal(barrier, inc=1, device_id={"tile": me + r}, device_id_type=MESH)

    own = REACH * rows
    for r in HOPS:
        @pl.when(jnp.logical_not(exists(me, r, n)))
        def _():
            t = r + REACH
            st_o[:, t * rows : (t + 1) * rows] = jnp.zeros((2, rows, SBLOCK), F32)
            codes_o[t] = jnp.full(codes_o.shape[1:], -1, jnp.int32)
    fetch_offs.wait()
    for k in range(rows):
        for w in range(2):
            st_o[w, own + k : own + k + 1] = offs[w : w + 1, k * SBLOCK : (k + 1) * SBLOCK]
    fetch_pairs.wait()

    peers = sum(exists(me, r, n).astype(jnp.int32) for r in HOPS)
    pl.semaphore_wait(barrier, peers)

    def copies(q, r):
        t = REACH - r
        made = []
        for which, (src, dst) in enumerate((
            (codes_o.at[REACH], codes_o.at[t]),
            (st_o.at[:, pl.ds(own, rows)], st_o.at[:, pl.ds(t * rows, rows)]),
        )):
            made.append(pltpu.make_async_remote_copy(
                src_ref=src, dst_ref=dst, send_sem=send_sem.at[which, q],
                recv_sem=recv_sem.at[which, q], device_id={"tile": me + r}, device_id_type=MESH,
            ))
        return made

    for q, r in enumerate(HOPS):
        @pl.when(exists(me, r, n))
        def _():
            for one in copies(q, r):
                one.start()

    fetch_band.wait()
    depth = (band[...].astype(F32) + 0.5) * (DEPTH_RANGE / BANDS)
    shifted = depth + DEPTH_SHIFT
    f_o[...] = (scale * STRETCH**3) * depth * (shifted * jnp.sqrt(shifted))
    q = lax.bitwise_and(lax.broadcasted_iota(jnp.int32, z_o.shape, 0), 3).astype(F32)
    z_o[...] = (STRETCH * STRETCH) * (depth * depth) + 0.25 * (q * q)

    def block(b, total):
        for q in range(CBLOCK // 128):
            lanes = pl.ds(pl.multiple_of(b * CBLOCK + q * 128, 128), 128)
            values = dirn[:, lanes]
            high, low = split(f_o[pl.ds(b * (CBLOCK // 128) + q, 1), :] * values)
            v_o[b, 0:16, q * 128 : (q + 1) * 128] = high
            v_o[b, 16:32, q * 128 : (q + 1) * 128] = low
            total = total + values * values
        return total

    total = jnp.zeros((dirn.shape[0], 128), F32)
    for k in range(CHUNKS):
        fetch_dirn[k].wait()
        total = lax.fori_loop(k * blocks // CHUNKS, (k + 1) * blocks // CHUNKS, block, total)
    norm_o[...] = jnp.broadcast_to(lane_sums(total), norm_o.shape)

    for q, r in enumerate(HOPS):
        @pl.when(exists(me, r, n))
        def _():
            for one in copies(q, r):
                one.wait_send()

        @pl.when(exists(me, -r, n))
        def _():
            for one in copies(q, r):
                one.wait_recv()

    codes = codes_o[...]
    slot = lax.broadcasted_iota(jnp.int32, codes.shape, 0)
    hit = lax.shift_right_arithmetic(codes, 5) == SPAN - 1 - slot
    slot = slot * rows + lax.broadcasted_iota(jnp.int32, codes.shape, 1)
    entries_o[...] = jnp.where(hit, slot * 32 + lax.bitwise_and(codes, 31), -1)


def fill_block(entry, slots, places, z, dst):
    j = lax.shift_right_logical(entry, 5)
    b = lax.bitwise_and(entry, 31)
    at = jnp.minimum(j, slots - 1)
    parity = lax.bitwise_and(b, 1).astype(F32)
    lane = lax.broadcasted_iota(jnp.int32, (8, 128), 1)
    unit = STRETCH / COL_SIDE
    cell_across = (lax.rem(lane, COL_SIDE).astype(F32) + 0.5) * unit
    cell_along = (lax.div(lane, COL_SIDE).astype(F32) + 0.5) * unit + (0.5 * STRETCH) * parity
    cell_across = jnp.concatenate([cell_across] * (STRIP // 8), axis=0)
    cell_along = jnp.concatenate([cell_along] * (STRIP // 8), axis=0)
    which = jnp.full((STRIP, 128), at, jnp.int32)
    deeps = [
        jnp.broadcast_to(z[pl.ds(b * (CBLOCK // 128) + q, 1), :], (8, 128))
        for q in range(CBLOCK // 128)
    ]
    for k in range(SBLOCK // STRIP):
        rows = slice(k * STRIP, (k + 1) * STRIP)
        across = jnp.take_along_axis(places[0, rows, :], which, axis=1) - cell_across
        along = jnp.take_along_axis(places[1, rows, :], which, axis=1) - cell_along
        flat = across * across + along * along
        for q in range(CBLOCK // 128):
            if q > 0:
                flat = flat - along
            inverse = lax.rsqrt(flat + jnp.concatenate([deeps[q]] * (STRIP // 8), axis=0))
            high, low = split(inverse * inverse * inverse)
            dst[0, q, rows, :] = high
            dst[1, q, rows, :] = low
    return j, b


def block_part(block, w):
    return jnp.concatenate([block[w, q] for q in range(CBLOCK // 128)], axis=1)


def forward_kernel(entries, st, z, v, img, pair_list, count, places, *rest):
    kept, spare = rest[:UNROLL], rest[UNROLL]
    slots = st.shape[1]
    pad = jnp.zeros((128 - slots, SBLOCK), F32)
    shift = lax.broadcasted_iota(jnp.int32, (slots, SBLOCK), 0) // entries.shape[1] - REACH
    places[0] = jnp.concatenate([STRETCH * (st[0] + shift.astype(F32)), pad], axis=0).T
    places[1] = jnp.concatenate([STRETCH * st[1], pad], axis=0).T
    rows = entries.shape[1]
    img[...] = jnp.zeros(img.shape, F32)
    nothing = SPAN * rows * 32
    pair_list[UNROLL - 1] = nothing
    filled = jnp.int32(UNROLL)
    for t in range(SPAN):
        def pick(row, filled):
            for p in range(entries.shape[2]):
                entry = entries[t, row, p]
                pair_list[filled] = entry
                filled = filled + (entry >= 0).astype(jnp.int32)
            return filled
        filled = lax.fori_loop(0, rows, pick, filled)
    for u in range(UNROLL):
        pair_list[filled + u] = nothing
    steps = (filled - 1) // UNROLL
    held = jnp.minimum(steps, KEPT // UNROLL)
    count[0] = steps
    count[1] = held

    def multiply(entry, block):
        j = lax.shift_right_logical(entry, 5)
        b = lax.bitwise_and(entry, 31)
        out = jnp.zeros((32, SBLOCK), F32)
        for w in range(2):
            out = out + lax.dot_general(
                v[b], block_part(block, w), (((1,), (1,)), ((), ())), preferred_element_type=F32
            )
        img[j] += out[0:16] + out[16:32]

    last = UNROLL - 1
    kept[last][0] = jnp.zeros(kept[last].shape[1:], BF16)

    def step(i, carry):
        at = (i + 1) * UNROLL
        for u in range(UNROLL):
            fill_block(pair_list[at + u], slots, places, z, kept[u].at[i])
            if u == 0:
                multiply(pair_list[at - 1], kept[last].at[jnp.maximum(i - 1, 0)])
            else:
                multiply(pair_list[at + u - 1], kept[u - 1].at[i])
        return carry

    def step_over(i, carry):
        for u in range(UNROLL):
            entry = pair_list[(i + 1) * UNROLL + u]
            fill_block(entry, slots, places, z, spare)
            multiply(entry, spare)
        return carry

    lax.fori_loop(0, held, step, 0)
    multiply(pair_list[held * UNROLL + last], kept[last].at[jnp.maximum(held - 1, 0)])
    lax.fori_loop(held, steps, step_over, 0)


def all_sum(n, me, mine, landing, send_sem, recv_sem, start, finish):
    def made(k):
        return pltpu.make_async_remote_copy(
            src_ref=mine, dst_ref=landing.at[k], send_sem=send_sem.at[k], recv_sem=recv_sem.at[k],
            device_id={"tile": lax.rem(me + k, n)}, device_id_type=MESH,
        )
    if start:
        def go(k, c):
            made(k).start()
            return c
        lax.fori_loop(1, n, go, 0)
    if finish:
        def done(k, c):
            made(k).wait()
            return c
        lax.fori_loop(1, n, done, 0)


def greet(n, me):
    barrier = pltpu.get_barrier_semaphore()

    def one(k, c):
        pl.semaphore_signal(
            barrier, inc=1, device_id={"tile": lax.rem(me + k, n)}, device_id_type=MESH
        )
        return c
    lax.fori_loop(1, n, one, 0)


def greeted(n):
    pl.semaphore_wait(pltpu.get_barrier_semaphore(), n - 1)


def image_kernel(
    n, rows, img, res_hbm, norm, old_hbm, newres_o, scal_o,
    res, old, in_sem, transit, joined, part_rx, norm_tx, norm_rx, send_sem, recv_sem, nsend_sem, nrecv_sem,
):
    me = lax.axis_index("tile")
    greet(n, me)
    fetch_old = pltpu.make_async_copy(old_hbm, old, in_sem.at[0])
    fetch_res = pltpu.make_async_copy(res_hbm, res, in_sem.at[1])
    fetch_old.start()
    fetch_res.start()
    greeted(n)
    s = 1 - 2 * lax.rem(me, 2)
    outward = exists(me, -2 * s, n)
    inward = exists(me, 2 * s, n)

    def slab(ref, r):
        return ref.at[pl.ds((REACH + r) * rows, rows)]

    def copy(number, src, dst, to):
        return pltpu.make_async_remote_copy(
            src_ref=src, dst_ref=dst, send_sem=send_sem.at[number],
            recv_sem=recv_sem.at[number], device_id={"tile": to}, device_id_type=MESH,
        )

    to_join = copy(0, slab(img, 2 * s), transit, me + s)
    to_sibling = copy(1, slab(img, s), part_rx.at[0], me + s)
    to_far = copy(2, slab(img, -2 * s), part_rx.at[1], me - 2 * s)
    to_near = copy(3, joined, part_rx.at[2], me - s)
    own = slab(newres_o, 0)
    give_near = copy(4, own, slab(newres_o, s), me - s)
    give_far = copy(5, own, slab(newres_o, -2 * s), me + 2 * s)
    give_sibling = copy(6, own, slab(newres_o, -s), me + s)
    pass_on = copy(7, slab(newres_o, -s), slab(newres_o, -2 * s), me + s)

    @pl.when(inward)
    def _():
        to_join.start()

    @pl.when(outward)
    def _():
        to_far.start()
    to_sibling.start()

    def squares(k, total):
        values = old[:, pl.ds(pl.multiple_of(k * 512, 512), 512)]
        return total + values * values

    fetch_old.wait()
    fetch_res.wait()
    before = lax.fori_loop(0, old.shape[1] // 512, squares, jnp.zeros((old.shape[0], 512), F32))
    lane = lax.broadcasted_iota(jnp.int32, (1, 128), 1)
    gamma_part = jnp.sum(lane_sums(before), axis=1, keepdims=True)
    norm_part = DAMPING * jnp.sum(norm[0:1, :], axis=1, keepdims=True)
    known = jnp.where(lane == 0, gamma_part, jnp.where(lane == 1, norm_part, 0.0))

    @pl.when(outward)
    def _():
        to_join.wait_recv()
        joined[...] = transit[...] + img[pl.ds((REACH - s) * rows, rows)]
        to_near.start()

    to_sibling.wait_recv()
    here = REACH * rows
    newres_o[here : here + rows] = img[here : here + rows] + part_rx[0]

    @pl.when(inward)
    def _():
        to_far.wait_recv()
        newres_o[here : here + rows] += part_rx[1]

    @pl.when(outward)
    def _():
        to_near.wait_recv()
        newres_o[here : here + rows] += part_rx[2]

    image = newres_o[here : here + rows]
    squared = lane_sums(jnp.sum(image * image, axis=0))
    folded = squared + jnp.where(lane == 1, 0.0, pltpu.roll(jnp.where(lane < 2, squared, 0.0), 2, 1))
    norm_tx[...] = jnp.where(lane < 2, known, folded)
    all_sum(n, me, norm_tx, norm_rx, nsend_sem, nrecv_sem, True, True)
    norm_rx[0] = norm_tx[...]
    totals = jnp.sum(norm_rx[...], axis=0)
    gamma_old = jnp.sum(jnp.where(lane == 0, totals, 0.0), axis=1, keepdims=True)
    curvature = jnp.sum(jnp.where(lane == 0, 0.0, totals), axis=1, keepdims=True)
    length = gamma_old / (curvature + GUARD)
    scal_o[...] = jnp.concatenate(
        [jnp.broadcast_to(length, (4, 128)), jnp.broadcast_to(gamma_old, (4, 128))], axis=0
    )
    for k in range(rows):
        newres_o[here + k] = res[:, k * SBLOCK : (k + 1) * SBLOCK] - length * newres_o[here + k]

    @pl.when(outward)
    def _():
        give_near.start()

    @pl.when(inward)
    def _():
        give_far.start()
    give_sibling.start()

    @pl.when(outward)
    def _():
        give_near.wait_recv()
        pass_on.start()
        to_far.wait_send()
        to_near.wait_send()
        give_far.wait_recv()
        give_near.wait_send()
        pass_on.wait_send()

    @pl.when(inward)
    def _():
        to_join.wait_send()
        give_far.wait_send()
        pass_on.wait_recv()
    to_sibling.wait_send()
    give_sibling.wait()


def adjoint_kernel(pair_list, count, places, z, newres, scal, model_in, dirn_in, *rest):
    kept = rest[:UNROLL]
    model_hbm, model_o, acc, res_o, dirn, parts, spare, in_sem, out_sem = rest[UNROLL:]
    slots = newres.shape[0]
    rows = slots // SPAN
    fetch_model = pltpu.make_async_copy(model_in, model_o, in_sem.at[0])
    fetch_dirn = pltpu.make_async_copy(dirn_in, dirn, in_sem.at[1])
    fetch_model.start()
    fetch_dirn.start()
    for k in range(rows):
        res_o[:, k * SBLOCK : (k + 1) * SBLOCK] = newres[REACH * rows + k]

    def cut(k, c):
        high, low = split(newres[k])
        parts[k, 0:16, :] = high
        parts[k, 16:32, :] = low
        return c
    lax.fori_loop(0, slots, cut, 0)
    parts[slots] = jnp.zeros((32, SBLOCK), BF16)
    acc[...] = jnp.zeros(acc.shape, F32)

    def add_pair(j, b, block):
        out = jnp.zeros((32, CBLOCK), F32)
        for w in range(2):
            out = out + jnp.dot(parts[j], block_part(block, w), preferred_element_type=F32)
        acc[b] += out[0:16] + out[16:32]

    def reread(i, carry):
        for u in range(UNROLL):
            entry = pair_list[(i + 1) * UNROLL + u]
            add_pair(lax.shift_right_logical(entry, 5), lax.bitwise_and(entry, 31), kept[u].at[i])
        return carry

    def rebuild(i, carry):
        for u in range(UNROLL):
            j, b = fill_block(pair_list[(i + 1) * UNROLL + u], slots, places, z, spare)
            add_pair(j, b, spare)
        return carry

    first = jnp.minimum(count[1], 1)
    lax.fori_loop(0, first, reread, 0)
    fetch_model.wait()
    fetch_dirn.wait()
    length = scal[0:1, 0:1]

    def update(b, c):
        lanes = pl.ds(pl.multiple_of(b * CBLOCK, CBLOCK), CBLOCK)
        model_o[:, lanes] = model_o[:, lanes] + length * dirn[:, lanes]
        return c
    lax.fori_loop(0, acc.shape[0], update, 0)
    leave = pltpu.make_async_copy(model_o, model_hbm, out_sem)
    leave.start()
    lax.fori_loop(first, count[1], reread, 0)
    lax.fori_loop(count[1], count[0], rebuild, 0)
    leave.wait()


def gamma_kernel(n, acc, model, f, scal, grad_o, ratio_o, mine, landing, send_sem, recv_sem):
    me = lax.axis_index("tile")
    greet(n, me)

    def finish(b, total):
        lanes = pl.ds(pl.multiple_of(b * CBLOCK, CBLOCK), CBLOCK)
        factor = jnp.concatenate(
            [f[pl.ds(b * (CBLOCK // 128) + q, 1), :] for q in range(CBLOCK // 128)], axis=1
        )
        gradient = factor * acc[b] - DAMPING * model[:, lanes]
        grad_o[:, lanes] = gradient
        return total + gradient * gradient

    total = lax.fori_loop(0, acc.shape[0], finish, jnp.zeros((model.shape[0], CBLOCK), F32))
    mine[...] = lane_sums(total)
    greeted(n)
    all_sum(n, me, mine, landing, send_sem, recv_sem, True, True)
    landing[0] = mine[...]
    total = jnp.sum(jnp.sum(landing[...], axis=0), axis=1, keepdims=True)
    ratio_o[...] = total / (scal[4:5, 0:1] + GUARD)


def shards(model_field, direction, old_grad, residual, block_pairs, depth_band, station_offsets):
    n = lax.axis_size("tile")
    epochs, cells = model_field.shape
    stations = residual.shape[1]
    rows = block_pairs.shape[0]
    pairs = block_pairs.shape[1]
    blocks = cells // CBLOCK
    scale = 2.0 / math.sqrt(cells)
    vmem = pl.BlockSpec(memory_space=pltpu.VMEM)
    smem = pl.BlockSpec(memory_space=pltpu.SMEM)
    hbm = pl.BlockSpec(memory_space=pltpu.HBM)
    shape = jax.ShapeDtypeStruct
    slots = SPAN * rows
    one_block = (2, CBLOCK // 128, SBLOCK, 128)
    dma = pltpu.SemaphoreType.DMA

    def in_hbm(one):
        return pltpu.with_memory_space_constraint(one, pltpu.HBM)

    def params(number=None):
        if number is None:
            return pltpu.CompilerParams(vmem_limit_bytes=VMEM_LIMIT)
        return pltpu.CompilerParams(
            vmem_limit_bytes=VMEM_LIMIT, collective_id=number, has_side_effects=True
        )

    st, entries, v, f, z, norm = pl.pallas_call(
        functools.partial(exchange_kernel, n, scale, blocks),
        out_shape=(
            shape((2, slots, SBLOCK), F32),
            shape((SPAN, rows, pairs), jnp.int32),
            shape((blocks, 2 * epochs, CBLOCK), BF16),
            shape((cells // 128, 128), F32),
            shape((cells // 128, 128), F32),
            shape((8, 128), F32),
        ),
        in_specs=[hbm] * 4,
        out_specs=(vmem,) * 6,
        scratch_shapes=[
            pltpu.VMEM((SPAN, rows, pairs), jnp.int32),
            pltpu.VMEM((epochs, cells), F32),
            pltpu.VMEM((cells // 128, 128), jnp.int32),
            pltpu.VMEM((2, stations), F32),
            dma((3 + CHUNKS,)),
            dma((2, len(HOPS))),
            dma((2, len(HOPS))),
        ],
        compiler_params=params(0),
        name="exchange",
    )(
        in_hbm(direction), in_hbm(block_pairs),
        in_hbm(depth_band.reshape(cells // 128, 128)), in_hbm(station_offsets),
    )

    img, pair_list, count, places, *kept = pl.pallas_call(
        forward_kernel,
        out_shape=(
            shape((slots + 1, epochs, SBLOCK), F32),
            shape((slots * pairs + 2 * UNROLL,), jnp.int32),
            shape((2,), jnp.int32),
            shape((2, SBLOCK, 128), F32),
        ) + (pltpu.VMEM((KEPT // UNROLL,) + one_block, BF16),) * UNROLL,
        in_specs=[smem, vmem, vmem, vmem],
        out_specs=(vmem, smem, smem) + (vmem,) * (1 + UNROLL),
        scratch_shapes=[pltpu.VMEM(one_block, BF16)],
        compiler_params=params(),
        name="forward",
    )(entries, st, z, v)

    kept = [pltpu.with_memory_space_constraint(one, pltpu.VMEM) for one in kept]
    newres, scal = pl.pallas_call(
        functools.partial(image_kernel, n, rows),
        out_shape=(shape((slots, epochs, SBLOCK), F32), shape((8, 128), F32)),
        in_specs=[vmem, hbm, vmem, hbm],
        out_specs=(vmem,) * 2,
        scratch_shapes=[
            pltpu.VMEM((epochs, stations), F32),
            pltpu.VMEM((epochs, cells), F32),
            dma((2,)),
            pltpu.VMEM((rows, epochs, SBLOCK), F32),
            pltpu.VMEM((rows, epochs, SBLOCK), F32),
            pltpu.VMEM((3, rows, epochs, SBLOCK), F32),
            pltpu.VMEM((1, 128), F32),
            pltpu.VMEM((n, 1, 128), F32),
            dma((8,)),
            dma((8,)),
            dma((n,)),
            dma((n,)),
        ],
        compiler_params=params(1),
        name="images",
    )(img, in_hbm(residual), norm, in_hbm(old_grad))

    new_model, model_kept, acc, new_residual = pl.pallas_call(
        adjoint_kernel,
        out_shape=(
            shape((epochs, cells), F32),
            shape((epochs, cells), F32),
            shape((blocks, epochs, CBLOCK), F32),
            shape((epochs, stations), F32),
        ),
        in_specs=[smem, smem] + [vmem] * 4 + [hbm] * 2 + [vmem] * UNROLL,
        out_specs=(hbm,) + (vmem,) * 3,
        scratch_shapes=[
            pltpu.VMEM((epochs, cells), F32),
            pltpu.VMEM((slots + 1, 2 * epochs, SBLOCK), BF16),
            pltpu.VMEM(one_block, BF16),
            dma((2,)),
            dma(()),
        ],
        compiler_params=params(),
        name="adjoint",
    )(
        pair_list, count, places, z, newres, scal, in_hbm(model_field), in_hbm(direction), *kept
    )

    gradient, ratio = pl.pallas_call(
        functools.partial(gamma_kernel, n),
        out_shape=(shape((epochs, cells), F32), shape((1, 1), F32)),
        in_specs=[vmem] * 4,
        out_specs=(vmem,) * 2,
        scratch_shapes=[
            pltpu.VMEM((1, 128), F32), pltpu.VMEM((n, 1, 128), F32), dma((n,)), dma((n,)),
        ],
        compiler_params=params(2),
        name="gamma",
    )(acc, model_kept, f, scal)
    new_direction = gradient + ratio.reshape(()) * direction
    return (new_model, new_residual, new_direction)


def solution(mesh):
    both = ("groups", "tile")
    wide = P(None, both)
    return jax.shard_map(
        shards,
        mesh=mesh,
        in_specs=(wide, wide, wide, wide, P(both, None), P(both), wide),
        out_specs=(wide, wide, wide),
        check_vma=False,
    )
```

```python
import functools
import math

import jax
import jax.numpy as jnp
from jax import lax
from jax.experimental import pallas as pl
from jax.experimental.pallas import tpu as pltpu
from jax.sharding import PartitionSpec as P

CBLOCK = 512
SBLOCK = 256
REACH = 2
BANDS = 16
COL_SIDE = 32
DEPTH_RANGE = 2.0
DEPTH_SHIFT = 0.25
DAMPING = 1.0
GUARD = 1e-06

SPAN = 2 * REACH + 1
CHUNKS = 4
HOPS = tuple(r for r in range(-REACH, REACH + 1) if r != 0)
UNROLL = 8
KEPT = 88
STRIP = 64
STRETCH = 4.0
MESH = pl.DeviceIdType.MESH
F32 = jnp.float32
BF16 = jnp.bfloat16
VMEM_LIMIT = 4 * 1024 * 1024


def exists(me, r, n):
    return jnp.logical_and(me + r >= 0, me + r < n)


def split(x):
    high = x.astype(BF16)
    return high, (x - high.astype(F32)).astype(BF16)


def lane_sums(x):
    total = jnp.sum(x, axis=0, keepdims=True)
    out = total[:, 0:128]
    for k in range(1, x.shape[1] // 128):
        out = out + total[:, k * 128 : (k + 1) * 128]
    return out


def exchange_kernel(
    n, scale, blocks, dirn_hbm, pairs, band_hbm, offs_hbm,
    st_o, entries_o, v_o, f_o, z_o, norm_o, codes_o,
    dirn, band, offs, in_sem, send_sem, recv_sem,
):
    me = lax.axis_index("tile")
    rows = pairs.shape[0]
    part = dirn.shape[1] // CHUNKS
    fetch_offs = pltpu.make_async_copy(offs_hbm, offs, in_sem.at[0])
    fetch_pairs = pltpu.make_async_copy(pairs, codes_o.at[REACH], in_sem.at[1])
    fetch_band = pltpu.make_async_copy(band_hbm, band, in_sem.at[2])
    fetch_dirn = [
        pltpu.make_async_copy(
            dirn_hbm.at[:, k * part : (k + 1) * part],
            dirn.at[:, k * part : (k + 1) * part],
            in_sem.at[3 + k],
        )
        for k in range(CHUNKS)
    ]
    for one in [fetch_offs, fetch_pairs, fetch_band] + fetch_dirn:
        one.start()
    barrier = pltpu.get_barrier_semaphore()
    for r in HOPS:
        @pl.when(exists(me, r, n))
        def _():
            pl.semaphore_signal(barrier, inc=1, device_id={"tile": me + r}, device_id_type=MESH)

    own = REACH * rows
    for r in HOPS:
        @pl.when(jnp.logical_not(exists(me, r, n)))
        def _():
            t = r + REACH
            st_o[:, t * rows : (t + 1) * rows] = jnp.zeros((2, rows, SBLOCK), F32)
            codes_o[t] = jnp.full(codes_o.shape[1:], -1, jnp.int32)
    fetch_offs.wait()
    for k in range(rows):
        for w in range(2):
            st_o[w, own + k : own + k + 1] = offs[w : w + 1, k * SBLOCK : (k + 1) * SBLOCK]
    fetch_pairs.wait()

    peers = sum(exists(me, r, n).astype(jnp.int32) for r in HOPS)
    pl.semaphore_wait(barrier, peers)

    def copies(q, r):
        t = REACH - r
        made = []
        for which, (src, dst) in enumerate((
            (codes_o.at[REACH], codes_o.at[t]),
            (st_o.at[:, pl.ds(own, rows)], st_o.at[:, pl.ds(t * rows, rows)]),
        )):
            made.append(pltpu.make_async_remote_copy(
                src_ref=src, dst_ref=dst, send_sem=send_sem.at[which, q],
                recv_sem=recv_sem.at[which, q], device_id={"tile": me + r}, device_id_type=MESH,
            ))
        return made

    for q, r in enumerate(HOPS):
        @pl.when(exists(me, r, n))
        def _():
            for one in copies(q, r):
                one.start()

    fetch_band.wait()
    depth = (band[...].astype(F32) + 0.5) * (DEPTH_RANGE / BANDS)
    shifted = depth + DEPTH_SHIFT
    f_o[...] = (scale * STRETCH**3) * depth * (shifted * jnp.sqrt(shifted))
    q = lax.bitwise_and(lax.broadcasted_iota(jnp.int32, z_o.shape, 0), 3).astype(F32)
    z_o[...] = (STRETCH * STRETCH) * (depth * depth) + 0.25 * (q * q)

    def block(b, total):
        for q in range(CBLOCK // 128):
            lanes = pl.ds(pl.multiple_of(b * CBLOCK + q * 128, 128), 128)
            values = dirn[:, lanes]
            high, low = split(f_o[pl.ds(b * (CBLOCK // 128) + q, 1), :] * values)
            v_o[b, 0:16, q * 128 : (q + 1) * 128] = high
            v_o[b, 16:32, q * 128 : (q + 1) * 128] = low
            total = total + values * values
        return total

    total = jnp.zeros((dirn.shape[0], 128), F32)
    for k in range(CHUNKS):
        fetch_dirn[k].wait()
        total = lax.fori_loop(k * blocks // CHUNKS, (k + 1) * blocks // CHUNKS, block, total)
    norm_o[...] = jnp.broadcast_to(lane_sums(total), norm_o.shape)

    for q, r in enumerate(HOPS):
        @pl.when(exists(me, r, n))
        def _():
            for one in copies(q, r):
                one.wait_send()

        @pl.when(exists(me, -r, n))
        def _():
            for one in copies(q, r):
                one.wait_recv()

    codes = codes_o[...]
    slot = lax.broadcasted_iota(jnp.int32, codes.shape, 0)
    hit = lax.shift_right_arithmetic(codes, 5) == SPAN - 1 - slot
    slot = slot * rows + lax.broadcasted_iota(jnp.int32, codes.shape, 1)
    entries_o[...] = jnp.where(hit, slot * 32 + lax.bitwise_and(codes, 31), -1)


def fill_block(entry, slots, places, z, dst):
    j = lax.shift_right_logical(entry, 5)
    b = lax.bitwise_and(entry, 31)
    at = jnp.minimum(j, slots - 1)
    parity = lax.bitwise_and(b, 1).astype(F32)
    lane = lax.broadcasted_iota(jnp.int32, (8, 128), 1)
    unit = STRETCH / COL_SIDE
    cell_across = (lax.rem(lane, COL_SIDE).astype(F32) + 0.5) * unit
    cell_along = (lax.div(lane, COL_SIDE).astype(F32) + 0.5) * unit + (0.5 * STRETCH) * parity
    cell_across = jnp.concatenate([cell_across] * (STRIP // 8), axis=0)
    cell_along = jnp.concatenate([cell_along] * (STRIP // 8), axis=0)
    which = jnp.full((STRIP, 128), at, jnp.int32)
    deeps = [
        jnp.broadcast_to(z[pl.ds(b * (CBLOCK // 128) + q, 1), :], (8, 128))
        for q in range(CBLOCK // 128)
    ]
    for k in range(SBLOCK // STRIP):
        rows = slice(k * STRIP, (k + 1) * STRIP)
        across = jnp.take_along_axis(places[0, rows, :], which, axis=1) - cell_across
        along = jnp.take_along_axis(places[1, rows, :], which, axis=1) - cell_along
        flat = across * across + along * along
        for q in range(CBLOCK // 128):
            if q > 0:
                flat = flat - along
            inverse = lax.rsqrt(flat + jnp.concatenate([deeps[q]] * (STRIP // 8), axis=0))
            high, low = split(inverse * inverse * inverse)
            dst[0, q, rows, :] = high
            dst[1, q, rows, :] = low
    return j, b


def block_part(block, w):
    return jnp.concatenate([block[w, q] for q in range(CBLOCK // 128)], axis=1)


def forward_kernel(entries_in, st, z, v, img, list_out, places, *rest):
    kept = rest[:UNROLL]
    spare, entries, pair_list, in_sem, out_sem = rest[UNROLL:]
    fetch = pltpu.make_async_copy(entries_in, entries, in_sem)
    fetch.start()
    slots = st.shape[1]
    pad = jnp.zeros((128 - slots, SBLOCK), F32)
    shift = lax.broadcasted_iota(jnp.int32, (slots, SBLOCK), 0) // entries.shape[1] - REACH
    places[0] = jnp.concatenate([STRETCH * (st[0] + shift.astype(F32)), pad], axis=0).T
    places[1] = jnp.concatenate([STRETCH * st[1], pad], axis=0).T
    rows = entries.shape[1]
    img[...] = jnp.zeros(img.shape, F32)
    last = UNROLL - 1
    kept[last][0] = jnp.zeros(kept[last].shape[1:], BF16)
    fetch.wait()
    nothing = SPAN * rows * 32
    pair_list[UNROLL - 1] = nothing
    filled = jnp.int32(UNROLL)
    for t in range(SPAN):
        def pick(row, filled):
            for p in range(entries.shape[2]):
                entry = entries[t, row, p]
                pair_list[filled] = entry
                filled = filled + (entry >= 0).astype(jnp.int32)
            return filled
        filled = lax.fori_loop(0, rows, pick, filled)
    for u in range(UNROLL):
        pair_list[filled + u] = nothing
    steps = (filled - 1) // UNROLL
    held = jnp.minimum(steps, KEPT // UNROLL)
    pair_list[0] = steps
    pair_list[1] = held
    leave = pltpu.make_async_copy(pair_list, list_out, out_sem)
    leave.start()

    def multiply(entry, block):
        j = lax.shift_right_logical(entry, 5)
        b = lax.bitwise_and(entry, 31)
        out = jnp.zeros((32, SBLOCK), F32)
        for w in range(2):
            out = out + lax.dot_general(
                v[b], block_part(block, w), (((1,), (1,)), ((), ())), preferred_element_type=F32
            )
        img[j] += out[0:16] + out[16:32]

    def step(i, carry):
        at = (i + 1) * UNROLL
        for u in range(UNROLL):
            fill_block(pair_list[at + u], slots, places, z, kept[u].at[i])
            if u == 0:
                multiply(pair_list[at - 1], kept[last].at[jnp.maximum(i - 1, 0)])
            else:
                multiply(pair_list[at + u - 1], kept[u - 1].at[i])
        return carry

    def step_over(i, carry):
        for u in range(UNROLL):
            entry = pair_list[(i + 1) * UNROLL + u]
            fill_block(entry, slots, places, z, spare)
            multiply(entry, spare)
        return carry

    lax.fori_loop(0, held, step, 0)
    multiply(pair_list[held * UNROLL + last], kept[last].at[jnp.maximum(held - 1, 0)])
    lax.fori_loop(held, steps, step_over, 0)
    leave.wait()


def all_sum(n, me, mine, landing, send_sem, recv_sem, start, finish):
    def made(k):
        return pltpu.make_async_remote_copy(
            src_ref=mine, dst_ref=landing.at[k], send_sem=send_sem.at[k], recv_sem=recv_sem.at[k],
            device_id={"tile": lax.rem(me + k, n)}, device_id_type=MESH,
        )
    if start:
        def go(k, c):
            made(k).start()
            return c
        lax.fori_loop(1, n, go, 0)
    if finish:
        def done(k, c):
            made(k).wait()
            return c
        lax.fori_loop(1, n, done, 0)


def greet(n, me):
    barrier = pltpu.get_barrier_semaphore()

    def one(k, c):
        pl.semaphore_signal(
            barrier, inc=1, device_id={"tile": lax.rem(me + k, n)}, device_id_type=MESH
        )
        return c
    lax.fori_loop(1, n, one, 0)


def greeted(n):
    pl.semaphore_wait(pltpu.get_barrier_semaphore(), n - 1)


def image_kernel(
    n, rows, img, res_hbm, norm, old_hbm, newres_o, scal_o,
    res, old, in_sem, transit, joined, part_rx, norm_tx, norm_rx, send_sem, recv_sem, nsend_sem, nrecv_sem,
):
    me = lax.axis_index("tile")
    greet(n, me)
    fetch_old = pltpu.make_async_copy(old_hbm, old, in_sem.at[0])
    fetch_res = pltpu.make_async_copy(res_hbm, res, in_sem.at[1])
    fetch_old.start()
    fetch_res.start()
    greeted(n)
    s = 1 - 2 * lax.rem(me, 2)
    outward = exists(me, -2 * s, n)
    inward = exists(me, 2 * s, n)

    def slab(ref, r):
        return ref.at[pl.ds((REACH + r) * rows, rows)]

    def copy(number, src, dst, to):
        return pltpu.make_async_remote_copy(
            src_ref=src, dst_ref=dst, send_sem=send_sem.at[number],
            recv_sem=recv_sem.at[number], device_id={"tile": to}, device_id_type=MESH,
        )

    to_join = copy(0, slab(img, 2 * s), transit, me + s)
    to_sibling = copy(1, slab(img, s), part_rx.at[0], me + s)
    to_far = copy(2, slab(img, -2 * s), part_rx.at[1], me - 2 * s)
    to_near = copy(3, joined, part_rx.at[2], me - s)
    own = slab(newres_o, 0)
    give_near = copy(4, own, slab(newres_o, s), me - s)
    give_far = copy(5, own, slab(newres_o, -2 * s), me + 2 * s)
    give_sibling = copy(6, own, slab(newres_o, -s), me + s)
    pass_on = copy(7, slab(newres_o, -s), slab(newres_o, -2 * s), me + s)

    @pl.when(inward)
    def _():
        to_join.start()

    @pl.when(outward)
    def _():
        to_far.start()
    to_sibling.start()

    def squares(k, total):
        values = old[:, pl.ds(pl.multiple_of(k * 512, 512), 512)]
        return total + values * values

    fetch_old.wait()
    fetch_res.wait()
    before = lax.fori_loop(0, old.shape[1] // 512, squares, jnp.zeros((old.shape[0], 512), F32))
    lane = lax.broadcasted_iota(jnp.int32, (1, 128), 1)
    gamma_part = jnp.sum(lane_sums(before), axis=1, keepdims=True)
    norm_part = DAMPING * jnp.sum(norm[0:1, :], axis=1, keepdims=True)
    known = jnp.where(lane == 0, gamma_part, jnp.where(lane == 1, norm_part, 0.0))

    @pl.when(outward)
    def _():
        to_join.wait_recv()
        joined[...] = transit[...] + img[pl.ds((REACH - s) * rows, rows)]
        to_near.start()

    to_sibling.wait_recv()
    here = REACH * rows
    newres_o[here : here + rows] = img[here : here + rows] + part_rx[0]

    @pl.when(inward)
    def _():
        to_far.wait_recv()
        newres_o[here : here + rows] += part_rx[1]

    @pl.when(outward)
    def _():
        to_near.wait_recv()
        newres_o[here : here + rows] += part_rx[2]

    image = newres_o[here : here + rows]
    squared = lane_sums(jnp.sum(image * image, axis=0))
    folded = squared + jnp.where(lane == 1, 0.0, pltpu.roll(jnp.where(lane < 2, squared, 0.0), 2, 1))
    norm_tx[...] = jnp.where(lane < 2, known, folded)
    all_sum(n, me, norm_tx, norm_rx, nsend_sem, nrecv_sem, True, True)
    norm_rx[0] = norm_tx[...]
    totals = jnp.sum(norm_rx[...], axis=0)
    gamma_old = jnp.sum(jnp.where(lane == 0, totals, 0.0), axis=1, keepdims=True)
    curvature = jnp.sum(jnp.where(lane == 0, 0.0, totals), axis=1, keepdims=True)
    length = gamma_old / (curvature + GUARD)
    scal_o[...] = jnp.concatenate(
        [jnp.broadcast_to(length, (4, 128)), jnp.broadcast_to(gamma_old, (4, 128))], axis=0
    )
    for k in range(rows):
        newres_o[here + k] = res[:, k * SBLOCK : (k + 1) * SBLOCK] - length * newres_o[here + k]

    @pl.when(outward)
    def _():
        give_near.start()

    @pl.when(inward)
    def _():
        give_far.start()
    give_sibling.start()

    @pl.when(outward)
    def _():
        give_near.wait_recv()
        pass_on.start()
        to_far.wait_send()
        to_near.wait_send()
        give_far.wait_recv()
        give_near.wait_send()
        pass_on.wait_send()

    @pl.when(inward)
    def _():
        to_join.wait_send()
        give_far.wait_send()
        pass_on.wait_recv()
    to_sibling.wait_send()
    give_sibling.wait()


def adjoint_kernel(list_in, places, z, newres, scal, model_in, dirn_in, *rest):
    kept = rest[:UNROLL]
    model_hbm, model_o, acc, res_hbm, pair_list, res_o, dirn, parts, spare, in_sem, out_sem = rest[UNROLL:]
    slots = newres.shape[0]
    rows = slots // SPAN
    fetch_model = pltpu.make_async_copy(model_in, model_o, in_sem.at[0])
    fetch_dirn = pltpu.make_async_copy(dirn_in, dirn, in_sem.at[1])
    fetch_list = pltpu.make_async_copy(list_in, pair_list, in_sem.at[2])
    fetch_list.start()
    fetch_model.start()
    fetch_dirn.start()
    for k in range(rows):
        res_o[:, k * SBLOCK : (k + 1) * SBLOCK] = newres[REACH * rows + k]
    leave_res = pltpu.make_async_copy(res_o, res_hbm, out_sem.at[1])
    leave_res.start()

    def cut(k, c):
        high, low = split(newres[k])
        parts[k, 0:16, :] = high
        parts[k, 16:32, :] = low
        return c
    lax.fori_loop(0, slots, cut, 0)
    parts[slots] = jnp.zeros((32, SBLOCK), BF16)
    acc[...] = jnp.zeros(acc.shape, F32)

    def add_pair(j, b, block):
        out = jnp.zeros((32, CBLOCK), F32)
        for w in range(2):
            out = out + jnp.dot(parts[j], block_part(block, w), preferred_element_type=F32)
        acc[b] += out[0:16] + out[16:32]

    def reread(i, carry):
        for u in range(UNROLL):
            entry = pair_list[(i + 1) * UNROLL + u]
            add_pair(lax.shift_right_logical(entry, 5), lax.bitwise_and(entry, 31), kept[u].at[i])
        return carry

    def rebuild(i, carry):
        for u in range(UNROLL):
            j, b = fill_block(pair_list[(i + 1) * UNROLL + u], slots, places, z, spare)
            add_pair(j, b, spare)
        return carry

    fetch_list.wait()
    steps = pair_list[0]
    held = pair_list[1]
    first = jnp.minimum(held, 1)
    lax.fori_loop(0, first, reread, 0)
    fetch_model.wait()
    fetch_dirn.wait()
    length = scal[0:1, 0:1]

    def update(b, c):
        lanes = pl.ds(pl.multiple_of(b * CBLOCK, CBLOCK), CBLOCK)
        model_o[:, lanes] = model_o[:, lanes] + length * dirn[:, lanes]
        return c
    lax.fori_loop(0, acc.shape[0], update, 0)
    leave = pltpu.make_async_copy(model_o, model_hbm, out_sem.at[0])
    leave.start()
    lax.fori_loop(first, held, reread, 0)
    lax.fori_loop(held, steps, rebuild, 0)
    leave_res.wait()
    leave.wait()


def gamma_kernel(n, acc, model, f, scal, grad_o, ratio_o, mine, landing, send_sem, recv_sem):
    me = lax.axis_index("tile")
    greet(n, me)

    def finish(b, total):
        lanes = pl.ds(pl.multiple_of(b * CBLOCK, CBLOCK), CBLOCK)
        factor = jnp.concatenate(
            [f[pl.ds(b * (CBLOCK // 128) + q, 1), :] for q in range(CBLOCK // 128)], axis=1
        )
        gradient = factor * acc[b] - DAMPING * model[:, lanes]
        grad_o[:, lanes] = gradient
        return total + gradient * gradient

    total = lax.fori_loop(0, acc.shape[0], finish, jnp.zeros((model.shape[0], CBLOCK), F32))
    mine[...] = lane_sums(total)
    greeted(n)
    all_sum(n, me, mine, landing, send_sem, recv_sem, True, True)
    landing[0] = mine[...]
    total = jnp.sum(jnp.sum(landing[...], axis=0), axis=1, keepdims=True)
    ratio_o[...] = total / (scal[4:5, 0:1] + GUARD)


def shards(model_field, direction, old_grad, residual, block_pairs, depth_band, station_offsets):
    n = lax.axis_size("tile")
    epochs, cells = model_field.shape
    stations = residual.shape[1]
    rows = block_pairs.shape[0]
    pairs = block_pairs.shape[1]
    blocks = cells // CBLOCK
    scale = 2.0 / math.sqrt(cells)
    vmem = pl.BlockSpec(memory_space=pltpu.VMEM)
    smem = pl.BlockSpec(memory_space=pltpu.SMEM)
    hbm = pl.BlockSpec(memory_space=pltpu.HBM)
    shape = jax.ShapeDtypeStruct
    slots = SPAN * rows
    listed = slots * pairs + 2 * UNROLL
    one_block = (2, CBLOCK // 128, SBLOCK, 128)
    dma = pltpu.SemaphoreType.DMA

    def in_hbm(one):
        return pltpu.with_memory_space_constraint(one, pltpu.HBM)

    def params(number=None):
        if number is None:
            return pltpu.CompilerParams(vmem_limit_bytes=VMEM_LIMIT)
        return pltpu.CompilerParams(
            vmem_limit_bytes=VMEM_LIMIT, collective_id=number, has_side_effects=True
        )

    st, entries, v, f, z, norm = pl.pallas_call(
        functools.partial(exchange_kernel, n, scale, blocks),
        out_shape=(
            shape((2, slots, SBLOCK), F32),
            shape((SPAN, rows, pairs), jnp.int32),
            shape((blocks, 2 * epochs, CBLOCK), BF16),
            shape((cells // 128, 128), F32),
            shape((cells // 128, 128), F32),
            shape((8, 128), F32),
        ),
        in_specs=[hbm] * 4,
        out_specs=(vmem,) * 6,
        scratch_shapes=[
            pltpu.VMEM((SPAN, rows, pairs), jnp.int32),
            pltpu.VMEM((epochs, cells), F32),
            pltpu.VMEM((cells // 128, 128), jnp.int32),
            pltpu.VMEM((2, stations), F32),
            dma((3 + CHUNKS,)),
            dma((2, len(HOPS))),
            dma((2, len(HOPS))),
        ],
        compiler_params=params(0),
        name="exchange",
    )(
        in_hbm(direction), in_hbm(block_pairs),
        in_hbm(depth_band.reshape(cells // 128, 128)), in_hbm(station_offsets),
    )

    img, pair_list, places, *kept = pl.pallas_call(
        forward_kernel,
        out_shape=(
            shape((slots + 1, epochs, SBLOCK), F32),
            shape((listed,), jnp.int32),
            shape((2, SBLOCK, 128), F32),
        ) + (pltpu.VMEM((KEPT // UNROLL,) + one_block, BF16),) * UNROLL,
        in_specs=[vmem] * 4,
        out_specs=(vmem, hbm) + (vmem,) * (1 + UNROLL),
        scratch_shapes=[
            pltpu.VMEM(one_block, BF16),
            pltpu.SMEM((SPAN, rows, pairs), jnp.int32),
            pltpu.SMEM((listed,), jnp.int32),
            dma(()),
            dma(()),
        ],
        compiler_params=params(),
        name="forward",
    )(entries, st, z, v)

    kept = [pltpu.with_memory_space_constraint(one, pltpu.VMEM) for one in kept]
    newres, scal = pl.pallas_call(
        functools.partial(image_kernel, n, rows),
        out_shape=(shape((slots, epochs, SBLOCK), F32), shape((8, 128), F32)),
        in_specs=[vmem, hbm, vmem, hbm],
        out_specs=(vmem,) * 2,
        scratch_shapes=[
            pltpu.VMEM((epochs, stations), F32),
            pltpu.VMEM((epochs, cells), F32),
            dma((2,)),
            pltpu.VMEM((rows, epochs, SBLOCK), F32),
            pltpu.VMEM((rows, epochs, SBLOCK), F32),
            pltpu.VMEM((3, rows, epochs, SBLOCK), F32),
            pltpu.VMEM((1, 128), F32),
            pltpu.VMEM((n, 1, 128), F32),
            dma((8,)),
            dma((8,)),
            dma((n,)),
            dma((n,)),
        ],
        compiler_params=params(1),
        name="images",
    )(img, in_hbm(residual), norm, in_hbm(old_grad))

    new_model, model_kept, acc, new_residual = pl.pallas_call(
        adjoint_kernel,
        out_shape=(
            shape((epochs, cells), F32),
            shape((epochs, cells), F32),
            shape((blocks, epochs, CBLOCK), F32),
            shape((epochs, stations), F32),
        ),
        in_specs=[pl.BlockSpec(memory_space=pl.ANY)] + [vmem] * 4 + [hbm] * 2 + [vmem] * UNROLL,
        out_specs=(hbm, vmem, vmem, hbm),
        scratch_shapes=[
            pltpu.SMEM((listed,), jnp.int32),
            pltpu.VMEM((epochs, stations), F32),
            pltpu.VMEM((epochs, cells), F32),
            pltpu.VMEM((slots + 1, 2 * epochs, SBLOCK), BF16),
            pltpu.VMEM(one_block, BF16),
            dma((3,)),
            dma((2,)),
        ],
        compiler_params=params(),
        name="adjoint",
    )(
        pair_list, places, z, newres, scal, in_hbm(model_field), in_hbm(direction), *kept
    )

    gradient, ratio = pl.pallas_call(
        functools.partial(gamma_kernel, n),
        out_shape=(shape((epochs, cells), F32), shape((1, 1), F32)),
        in_specs=[vmem] * 4,
        out_specs=(vmem,) * 2,
        scratch_shapes=[
            pltpu.VMEM((1, 128), F32), pltpu.VMEM((n, 1, 128), F32), dma((n,)), dma((n,)),
        ],
        compiler_params=params(2),
        name="gamma",
    )(acc, model_kept, f, scal)
    new_direction = gradient + ratio.reshape(()) * direction
    return (new_model, new_residual, new_direction)


def solution(mesh):
    both = ("groups", "tile")
    wide = P(None, both)
    return jax.shard_map(
        shards,
        mesh=mesh,
        in_specs=(wide, wide, wide, wide, P(both, None), P(both), wide),
        out_specs=(wide, wide, wide),
        check_vma=False,
    )
```

```python
import functools
import math

import jax
import jax.numpy as jnp
from jax import lax
from jax.experimental import pallas as pl
from jax.experimental.pallas import tpu as pltpu
from jax.sharding import PartitionSpec as P

CBLOCK = 512
SBLOCK = 256
REACH = 2
BANDS = 16
COL_SIDE = 32
DEPTH_RANGE = 2.0
DEPTH_SHIFT = 0.25
DAMPING = 1.0
GUARD = 1e-06

SPAN = 2 * REACH + 1
CHUNKS = 4
HOPS = tuple(r for r in range(-REACH, REACH + 1) if r != 0)
UNROLL = 8
KEPT = 88
LAG = 2
STRIP = 64
STRETCH = 4.0
MESH = pl.DeviceIdType.MESH
F32 = jnp.float32
BF16 = jnp.bfloat16
VMEM_LIMIT = 4 * 1024 * 1024


def in_groups(size, body, start):
    group = math.gcd(size, 4)

    def several(k, carry):
        for m in range(group):
            carry = body(k * group + m, carry)
        return carry
    return lax.fori_loop(0, size // group, several, start)


def exists(me, r, n):
    return jnp.logical_and(me + r >= 0, me + r < n)


def split(x):
    high = x.astype(BF16)
    return high, (x - high.astype(F32)).astype(BF16)


def lane_sums(x):
    total = jnp.sum(x, axis=0, keepdims=True)
    out = total[:, 0:128]
    for k in range(1, x.shape[1] // 128):
        out = out + total[:, k * 128 : (k + 1) * 128]
    return out


def exchange_kernel(
    n, scale, blocks, dirn_hbm, pairs, band_hbm, offs_hbm,
    st_o, entries_o, v_o, f_o, z_o, norm_o, codes_o,
    dirn, band, offs, in_sem, send_sem, recv_sem,
):
    me = lax.axis_index("tile")
    rows = pairs.shape[0]
    part = dirn.shape[1] // CHUNKS
    fetch_offs = pltpu.make_async_copy(offs_hbm, offs, in_sem.at[0])
    fetch_pairs = pltpu.make_async_copy(pairs, codes_o.at[REACH], in_sem.at[1])
    fetch_band = pltpu.make_async_copy(band_hbm, band, in_sem.at[2])
    fetch_dirn = [
        pltpu.make_async_copy(
            dirn_hbm.at[:, k * part : (k + 1) * part],
            dirn.at[:, k * part : (k + 1) * part],
            in_sem.at[3 + k],
        )
        for k in range(CHUNKS)
    ]
    for one in [fetch_offs, fetch_pairs, fetch_band] + fetch_dirn:
        one.start()
    barrier = pltpu.get_barrier_semaphore()
    for r in HOPS:
        @pl.when(exists(me, r, n))
        def _():
            pl.semaphore_signal(barrier, inc=1, device_id={"tile": me + r}, device_id_type=MESH)

    own = REACH * rows
    for r in HOPS:
        @pl.when(jnp.logical_not(exists(me, r, n)))
        def _():
            t = r + REACH
            st_o[:, t * rows : (t + 1) * rows] = jnp.zeros((2, rows, SBLOCK), F32)
            codes_o[t] = jnp.full(codes_o.shape[1:], -1, jnp.int32)
    fetch_offs.wait()
    for k in range(rows):
        for w in range(2):
            st_o[w, own + k : own + k + 1] = offs[w : w + 1, k * SBLOCK : (k + 1) * SBLOCK]
    fetch_pairs.wait()

    peers = sum(exists(me, r, n).astype(jnp.int32) for r in HOPS)
    pl.semaphore_wait(barrier, peers)

    def copies(q, r):
        t = REACH - r
        made = []
        for which, (src, dst) in enumerate((
            (codes_o.at[REACH], codes_o.at[t]),
            (st_o.at[:, pl.ds(own, rows)], st_o.at[:, pl.ds(t * rows, rows)]),
        )):
            made.append(pltpu.make_async_remote_copy(
                src_ref=src, dst_ref=dst, send_sem=send_sem.at[which, q],
                recv_sem=recv_sem.at[which, q], device_id={"tile": me + r}, device_id_type=MESH,
            ))
        return made

    for q, r in enumerate(HOPS):
        @pl.when(exists(me, r, n))
        def _():
            for one in copies(q, r):
                one.start()

    fetch_band.wait()
    depth = (band[...].astype(F32) + 0.5) * (DEPTH_RANGE / BANDS)
    shifted = depth + DEPTH_SHIFT
    f_o[...] = (scale * STRETCH**3) * depth * (shifted * jnp.sqrt(shifted))
    q = lax.bitwise_and(lax.broadcasted_iota(jnp.int32, z_o.shape, 0), 3).astype(F32)
    z_o[...] = (STRETCH * STRETCH) * (depth * depth) + 0.25 * (q * q)

    def block(first, b, total):
        b = first + b
        for q in range(CBLOCK // 128):
            lanes = pl.ds(pl.multiple_of(b * CBLOCK + q * 128, 128), 128)
            values = dirn[:, lanes]
            high, low = split(f_o[pl.ds(b * (CBLOCK // 128) + q, 1), :] * values)
            v_o[b, 0:16, q * 128 : (q + 1) * 128] = high
            v_o[b, 16:32, q * 128 : (q + 1) * 128] = low
            total = total + values * values
        return total

    total = jnp.zeros((dirn.shape[0], 128), F32)
    for k in range(CHUNKS):
        fetch_dirn[k].wait()
        total = in_groups(blocks // CHUNKS, functools.partial(block, k * blocks // CHUNKS), total)
    norm_o[...] = jnp.broadcast_to(lane_sums(total), norm_o.shape)

    for q, r in enumerate(HOPS):
        @pl.when(exists(me, r, n))
        def _():
            for one in copies(q, r):
                one.wait_send()

        @pl.when(exists(me, -r, n))
        def _():
            for one in copies(q, r):
                one.wait_recv()

    codes = codes_o[...]
    slot = lax.broadcasted_iota(jnp.int32, codes.shape, 0)
    hit = lax.shift_right_arithmetic(codes, 5) == SPAN - 1 - slot
    slot = slot * rows + lax.broadcasted_iota(jnp.int32, codes.shape, 1)
    entries_o[...] = jnp.where(hit, slot * 32 + lax.bitwise_and(codes, 31), -1)


def fill_block(entry, slots, places, z, dst):
    j = lax.shift_right_logical(entry, 5)
    b = lax.bitwise_and(entry, 31)
    at = jnp.minimum(j, slots - 1)
    parity = lax.bitwise_and(b, 1).astype(F32)
    lane = lax.broadcasted_iota(jnp.int32, (8, 128), 1)
    unit = STRETCH / COL_SIDE
    cell_across = (lax.rem(lane, COL_SIDE).astype(F32) + 0.5) * unit
    cell_along = (lax.div(lane, COL_SIDE).astype(F32) + 0.5) * unit + (0.5 * STRETCH) * parity
    cell_across = jnp.concatenate([cell_across] * (STRIP // 8), axis=0)
    cell_along = jnp.concatenate([cell_along] * (STRIP // 8), axis=0)
    which = jnp.full((STRIP, 128), at, jnp.int32)
    deeps = [
        jnp.broadcast_to(z[pl.ds(b * (CBLOCK // 128) + q, 1), :], (8, 128))
        for q in range(CBLOCK // 128)
    ]
    for k in range(SBLOCK // STRIP):
        rows = slice(k * STRIP, (k + 1) * STRIP)
        across = jnp.take_along_axis(places[0, rows, :], which, axis=1) - cell_across
        along = jnp.take_along_axis(places[1, rows, :], which, axis=1) - cell_along
        flat = across * across + along * along
        for q in range(CBLOCK // 128):
            if q > 0:
                flat = flat - along
            inverse = lax.rsqrt(flat + jnp.concatenate([deeps[q]] * (STRIP // 8), axis=0))
            high, low = split(inverse * inverse * inverse)
            dst[0, q, rows, :] = high
            dst[1, q, rows, :] = low
    return j, b


def block_part(block, w):
    return jnp.concatenate([block[w, q] for q in range(CBLOCK // 128)], axis=1)


def forward_kernel(entries_in, st, z, v, img, list_out, places, *rest):
    kept = rest[:UNROLL]
    spare, entries, pair_list, in_sem, out_sem = rest[UNROLL:]
    fetch = pltpu.make_async_copy(entries_in, entries, in_sem)
    fetch.start()
    slots = st.shape[1]
    pad = jnp.zeros((128 - slots, SBLOCK), F32)
    shift = lax.broadcasted_iota(jnp.int32, (slots, SBLOCK), 0) // entries.shape[1] - REACH
    places[0] = jnp.concatenate([STRETCH * (st[0] + shift.astype(F32)), pad], axis=0).T
    places[1] = jnp.concatenate([STRETCH * st[1], pad], axis=0).T
    rows = entries.shape[1]
    img[...] = jnp.zeros(img.shape, F32)
    for u in range(UNROLL - LAG, UNROLL):
        kept[u][0] = jnp.zeros(kept[u].shape[1:], BF16)
    fetch.wait()
    nothing = SPAN * rows * 32
    for u in range(UNROLL - LAG, UNROLL):
        pair_list[u] = nothing
    filled = jnp.int32(UNROLL)
    for t in range(SPAN):
        def pick(row, filled):
            for p in range(entries.shape[2]):
                entry = entries[t, row, p]
                pair_list[filled] = entry
                filled = filled + (entry >= 0).astype(jnp.int32)
            return filled
        filled = lax.fori_loop(0, rows, pick, filled)
    for u in range(UNROLL):
        pair_list[filled + u] = nothing
    steps = (filled - 1) // UNROLL
    held = jnp.minimum(steps, KEPT // UNROLL)
    pair_list[0] = steps
    pair_list[1] = held
    leave = pltpu.make_async_copy(pair_list, list_out, out_sem)
    leave.start()

    def multiply(entry, block):
        j = lax.shift_right_logical(entry, 5)
        b = lax.bitwise_and(entry, 31)
        out = jnp.zeros((32, SBLOCK), F32)
        for w in range(2):
            out = out + lax.dot_general(
                v[b], block_part(block, w), (((1,), (1,)), ((), ())), preferred_element_type=F32
            )
        img[j] += out[0:16] + out[16:32]

    def step(i, carry):
        at = (i + 1) * UNROLL
        for u in range(UNROLL):
            fill_block(pair_list[at + u], slots, places, z, kept[u].at[i])
            if u < LAG:
                earlier = kept[UNROLL + u - LAG].at[jnp.maximum(i - 1, 0)]
            else:
                earlier = kept[u - LAG].at[i]
            multiply(pair_list[at + u - LAG], earlier)
        return carry

    def step_over(i, carry):
        for u in range(UNROLL):
            entry = pair_list[(i + 1) * UNROLL + u]
            fill_block(entry, slots, places, z, spare)
            multiply(entry, spare)
        return carry

    lax.fori_loop(0, held, step, 0)
    for u in range(UNROLL - LAG, UNROLL):
        multiply(pair_list[held * UNROLL + u], kept[u].at[jnp.maximum(held - 1, 0)])
    lax.fori_loop(held, steps, step_over, 0)
    leave.wait()


def all_sum(n, me, mine, landing, send_sem, recv_sem, start, finish):
    def made(k):
        return pltpu.make_async_remote_copy(
            src_ref=mine, dst_ref=landing.at[k], send_sem=send_sem.at[k], recv_sem=recv_sem.at[k],
            device_id={"tile": lax.rem(me + k, n)}, device_id_type=MESH,
        )
    if start:
        def go(k, c):
            made(k).start()
            return c
        lax.fori_loop(1, n, go, 0)
    if finish:
        def done(k, c):
            made(k).wait()
            return c
        lax.fori_loop(1, n, done, 0)


def greet(n, me):
    barrier = pltpu.get_barrier_semaphore()

    def one(k, c):
        pl.semaphore_signal(
            barrier, inc=1, device_id={"tile": lax.rem(me + k, n)}, device_id_type=MESH
        )
        return c
    lax.fori_loop(1, n, one, 0)


def greeted(n):
    pl.semaphore_wait(pltpu.get_barrier_semaphore(), n - 1)


def image_kernel(
    n, rows, img, res_hbm, norm, old_hbm, newres_o, scal_o,
    res, old, in_sem, transit, joined, part_rx, norm_tx, norm_rx, send_sem, recv_sem, nsend_sem, nrecv_sem,
):
    me = lax.axis_index("tile")
    greet(n, me)
    fetch_old = pltpu.make_async_copy(old_hbm, old, in_sem.at[0])
    fetch_res = pltpu.make_async_copy(res_hbm, res, in_sem.at[1])
    fetch_old.start()
    fetch_res.start()
    greeted(n)
    s = 1 - 2 * lax.rem(me, 2)
    outward = exists(me, -2 * s, n)
    inward = exists(me, 2 * s, n)

    def slab(ref, r):
        return ref.at[pl.ds((REACH + r) * rows, rows)]

    def copy(number, src, dst, to):
        return pltpu.make_async_remote_copy(
            src_ref=src, dst_ref=dst, send_sem=send_sem.at[number],
            recv_sem=recv_sem.at[number], device_id={"tile": to}, device_id_type=MESH,
        )

    to_join = copy(0, slab(img, 2 * s), transit, me + s)
    to_sibling = copy(1, slab(img, s), part_rx.at[0], me + s)
    to_far = copy(2, slab(img, -2 * s), part_rx.at[1], me - 2 * s)
    to_near = copy(3, joined, part_rx.at[2], me - s)
    own = slab(newres_o, 0)
    give_near = copy(4, own, slab(newres_o, s), me - s)
    give_far = copy(5, own, slab(newres_o, -2 * s), me + 2 * s)
    give_sibling = copy(6, own, slab(newres_o, -s), me + s)
    pass_on = copy(7, slab(newres_o, -s), slab(newres_o, -2 * s), me + s)

    @pl.when(inward)
    def _():
        to_join.start()

    @pl.when(outward)
    def _():
        to_far.start()
    to_sibling.start()

    def squares(k, total):
        values = old[:, pl.ds(pl.multiple_of(k * 512, 512), 512)]
        return total + values * values

    fetch_old.wait()
    fetch_res.wait()
    before = in_groups(old.shape[1] // 512, squares, jnp.zeros((old.shape[0], 512), F32))
    lane = lax.broadcasted_iota(jnp.int32, (1, 128), 1)
    gamma_part = jnp.sum(lane_sums(before), axis=1, keepdims=True)
    norm_part = DAMPING * jnp.sum(norm[0:1, :], axis=1, keepdims=True)
    known = jnp.where(lane == 0, gamma_part, jnp.where(lane == 1, norm_part, 0.0))

    @pl.when(outward)
    def _():
        to_join.wait_recv()
        joined[...] = transit[...] + img[pl.ds((REACH - s) * rows, rows)]
        to_near.start()

    to_sibling.wait_recv()
    here = REACH * rows
    newres_o[here : here + rows] = img[here : here + rows] + part_rx[0]

    @pl.when(inward)
    def _():
        to_far.wait_recv()
        newres_o[here : here + rows] += part_rx[1]

    @pl.when(outward)
    def _():
        to_near.wait_recv()
        newres_o[here : here + rows] += part_rx[2]

    image = newres_o[here : here + rows]
    squared = lane_sums(jnp.sum(image * image, axis=0))
    folded = squared + jnp.where(lane == 1, 0.0, pltpu.roll(jnp.where(lane < 2, squared, 0.0), 2, 1))
    norm_tx[...] = jnp.where(lane < 2, known, folded)
    all_sum(n, me, norm_tx, norm_rx, nsend_sem, nrecv_sem, True, True)
    norm_rx[0] = norm_tx[...]
    totals = jnp.sum(norm_rx[...], axis=0)
    gamma_old = jnp.sum(jnp.where(lane == 0, totals, 0.0), axis=1, keepdims=True)
    curvature = jnp.sum(jnp.where(lane == 0, 0.0, totals), axis=1, keepdims=True)
    length = gamma_old / (curvature + GUARD)
    scal_o[...] = jnp.concatenate(
        [jnp.broadcast_to(length, (4, 128)), jnp.broadcast_to(gamma_old, (4, 128))], axis=0
    )
    for k in range(rows):
        newres_o[here + k] = res[:, k * SBLOCK : (k + 1) * SBLOCK] - length * newres_o[here + k]

    @pl.when(outward)
    def _():
        give_near.start()

    @pl.when(inward)
    def _():
        give_far.start()
    give_sibling.start()

    @pl.when(outward)
    def _():
        give_near.wait_recv()
        pass_on.start()
        to_far.wait_send()
        to_near.wait_send()
        give_far.wait_recv()
        give_near.wait_send()
        pass_on.wait_send()

    @pl.when(inward)
    def _():
        to_join.wait_send()
        give_far.wait_send()
        pass_on.wait_recv()
    to_sibling.wait_send()
    give_sibling.wait()


def adjoint_kernel(list_in, places, z, newres, scal, model_in, dirn_in, *rest):
    kept = rest[:UNROLL]
    model_hbm, model_o, acc, res_hbm, pair_list, res_o, dirn, parts, spare, in_sem, out_sem = rest[UNROLL:]
    slots = newres.shape[0]
    rows = slots // SPAN
    fetch_model = pltpu.make_async_copy(model_in, model_o, in_sem.at[0])
    fetch_dirn = pltpu.make_async_copy(dirn_in, dirn, in_sem.at[1])
    fetch_list = pltpu.make_async_copy(list_in, pair_list, in_sem.at[2])
    fetch_list.start()
    fetch_model.start()
    fetch_dirn.start()
    for k in range(rows):
        res_o[:, k * SBLOCK : (k + 1) * SBLOCK] = newres[REACH * rows + k]
    leave_res = pltpu.make_async_copy(res_o, res_hbm, out_sem.at[1])
    leave_res.start()

    def cut(k, c):
        high, low = split(newres[k])
        parts[k, 0:16, :] = high
        parts[k, 16:32, :] = low
        return c
    in_groups(slots, cut, 0)
    parts[slots] = jnp.zeros((32, SBLOCK), BF16)
    acc[...] = jnp.zeros(acc.shape, F32)

    def add_pair(j, b, block):
        out = jnp.zeros((32, CBLOCK), F32)
        for w in range(2):
            out = out + jnp.dot(parts[j], block_part(block, w), preferred_element_type=F32)
        acc[b] += out[0:16] + out[16:32]

    def reread(i, carry):
        for u in range(UNROLL):
            entry = pair_list[(i + 1) * UNROLL + u]
            add_pair(lax.shift_right_logical(entry, 5), lax.bitwise_and(entry, 31), kept[u].at[i])
        return carry

    def rebuild(i, carry):
        for u in range(UNROLL):
            j, b = fill_block(pair_list[(i + 1) * UNROLL + u], slots, places, z, spare)
            add_pair(j, b, spare)
        return carry

    fetch_list.wait()
    steps = pair_list[0]
    held = pair_list[1]
    first = jnp.minimum(held, 1)
    lax.fori_loop(0, first, reread, 0)
    fetch_model.wait()
    fetch_dirn.wait()
    length = scal[0:1, 0:1]

    def update(b, c):
        lanes = pl.ds(pl.multiple_of(b * CBLOCK, CBLOCK), CBLOCK)
        model_o[:, lanes] = model_o[:, lanes] + length * dirn[:, lanes]
        return c
    in_groups(acc.shape[0], update, 0)
    leave = pltpu.make_async_copy(model_o, model_hbm, out_sem.at[0])
    leave.start()
    lax.fori_loop(first, held, reread, 0)
    lax.fori_loop(held, steps, rebuild, 0)
    leave_res.wait()
    leave.wait()


def gamma_kernel(n, acc, model, f, scal, grad_o, ratio_o, mine, landing, send_sem, recv_sem):
    me = lax.axis_index("tile")
    greet(n, me)

    def finish(b, total):
        lanes = pl.ds(pl.multiple_of(b * CBLOCK, CBLOCK), CBLOCK)
        factor = jnp.concatenate(
            [f[pl.ds(b * (CBLOCK // 128) + q, 1), :] for q in range(CBLOCK // 128)], axis=1
        )
        gradient = factor * acc[b] - DAMPING * model[:, lanes]
        grad_o[:, lanes] = gradient
        return total + gradient * gradient

    total = in_groups(acc.shape[0], finish, jnp.zeros((model.shape[0], CBLOCK), F32))
    mine[...] = lane_sums(total)
    greeted(n)
    all_sum(n, me, mine, landing, send_sem, recv_sem, True, True)
    landing[0] = mine[...]
    total = jnp.sum(jnp.sum(landing[...], axis=0), axis=1, keepdims=True)
    ratio_o[...] = total / (scal[4:5, 0:1] + GUARD)


def shards(model_field, direction, old_grad, residual, block_pairs, depth_band, station_offsets):
    n = lax.axis_size("tile")
    epochs, cells = model_field.shape
    stations = residual.shape[1]
    rows = block_pairs.shape[0]
    pairs = block_pairs.shape[1]
    blocks = cells // CBLOCK
    scale = 2.0 / math.sqrt(cells)
    vmem = pl.BlockSpec(memory_space=pltpu.VMEM)
    smem = pl.BlockSpec(memory_space=pltpu.SMEM)
    hbm = pl.BlockSpec(memory_space=pltpu.HBM)
    shape = jax.ShapeDtypeStruct
    slots = SPAN * rows
    listed = slots * pairs + 2 * UNROLL
    one_block = (2, CBLOCK // 128, SBLOCK, 128)
    dma = pltpu.SemaphoreType.DMA

    def in_hbm(one):
        return pltpu.with_memory_space_constraint(one, pltpu.HBM)

    def params(number=None):
        if number is None:
            return pltpu.CompilerParams(vmem_limit_bytes=VMEM_LIMIT)
        return pltpu.CompilerParams(
            vmem_limit_bytes=VMEM_LIMIT, collective_id=number, has_side_effects=True
        )

    st, entries, v, f, z, norm = pl.pallas_call(
        functools.partial(exchange_kernel, n, scale, blocks),
        out_shape=(
            shape((2, slots, SBLOCK), F32),
            shape((SPAN, rows, pairs), jnp.int32),
            shape((blocks, 2 * epochs, CBLOCK), BF16),
            shape((cells // 128, 128), F32),
            shape((cells // 128, 128), F32),
            shape((8, 128), F32),
        ),
        in_specs=[hbm] * 4,
        out_specs=(vmem,) * 6,
        scratch_shapes=[
            pltpu.VMEM((SPAN, rows, pairs), jnp.int32),
            pltpu.VMEM((epochs, cells), F32),
            pltpu.VMEM((cells // 128, 128), jnp.int32),
            pltpu.VMEM((2, stations), F32),
            dma((3 + CHUNKS,)),
            dma((2, len(HOPS))),
            dma((2, len(HOPS))),
        ],
        compiler_params=params(0),
        name="exchange",
    )(
        in_hbm(direction), in_hbm(block_pairs),
        in_hbm(depth_band.reshape(cells // 128, 128)), in_hbm(station_offsets),
    )

    img, pair_list, places, *kept = pl.pallas_call(
        forward_kernel,
        out_shape=(
            shape((slots + 1, epochs, SBLOCK), F32),
            shape((listed,), jnp.int32),
            shape((2, SBLOCK, 128), F32),
        ) + (pltpu.VMEM((KEPT // UNROLL,) + one_block, BF16),) * UNROLL,
        in_specs=[vmem] * 4,
        out_specs=(vmem, hbm) + (vmem,) * (1 + UNROLL),
        scratch_shapes=[
            pltpu.VMEM(one_block, BF16),
            pltpu.SMEM((SPAN, rows, pairs), jnp.int32),
            pltpu.SMEM((listed,), jnp.int32),
            dma(()),
            dma(()),
        ],
        compiler_params=params(),
        name="forward",
    )(entries, st, z, v)

    kept = [pltpu.with_memory_space_constraint(one, pltpu.VMEM) for one in kept]
    newres, scal = pl.pallas_call(
        functools.partial(image_kernel, n, rows),
        out_shape=(shape((slots, epochs, SBLOCK), F32), shape((8, 128), F32)),
        in_specs=[vmem, hbm, vmem, hbm],
        out_specs=(vmem,) * 2,
        scratch_shapes=[
            pltpu.VMEM((epochs, stations), F32),
            pltpu.VMEM((epochs, cells), F32),
            dma((2,)),
            pltpu.VMEM((rows, epochs, SBLOCK), F32),
            pltpu.VMEM((rows, epochs, SBLOCK), F32),
            pltpu.VMEM((3, rows, epochs, SBLOCK), F32),
            pltpu.VMEM((1, 128), F32),
            pltpu.VMEM((n, 1, 128), F32),
            dma((8,)),
            dma((8,)),
            dma((n,)),
            dma((n,)),
        ],
        compiler_params=params(1),
        name="images",
    )(img, in_hbm(residual), norm, in_hbm(old_grad))

    new_model, model_kept, acc, new_residual = pl.pallas_call(
        adjoint_kernel,
        out_shape=(
            shape((epochs, cells), F32),
            shape((epochs, cells), F32),
            shape((blocks, epochs, CBLOCK), F32),
            shape((epochs, stations), F32),
        ),
        in_specs=[pl.BlockSpec(memory_space=pl.ANY)] + [vmem] * 4 + [hbm] * 2 + [vmem] * UNROLL,
        out_specs=(hbm, vmem, vmem, hbm),
        scratch_shapes=[
            pltpu.SMEM((listed,), jnp.int32),
            pltpu.VMEM((epochs, stations), F32),
            pltpu.VMEM((epochs, cells), F32),
            pltpu.VMEM((slots + 1, 2 * epochs, SBLOCK), BF16),
            pltpu.VMEM(one_block, BF16),
            dma((3,)),
            dma((2,)),
        ],
        compiler_params=params(),
        name="adjoint",
    )(
        pair_list, places, z, newres, scal, in_hbm(model_field), in_hbm(direction), *kept
    )

    gradient, ratio = pl.pallas_call(
        functools.partial(gamma_kernel, n),
        out_shape=(shape((epochs, cells), F32), shape((1, 1), F32)),
        in_specs=[vmem] * 4,
        out_specs=(vmem,) * 2,
        scratch_shapes=[
            pltpu.VMEM((1, 128), F32), pltpu.VMEM((n, 1, 128), F32), dma((n,)), dma((n,)),
        ],
        compiler_params=params(2),
        name="gamma",
    )(acc, model_kept, f, scal)
    new_direction = gradient + ratio.reshape(()) * direction
    return (new_model, new_residual, new_direction)


def solution(mesh):
    both = ("groups", "tile")
    wide = P(None, both)
    return jax.shard_map(
        shards,
        mesh=mesh,
        in_specs=(wide, wide, wide, wide, P(both, None), P(both), wide),
        out_specs=(wide, wide, wide),
        check_vma=False,
    )
```

```python
import functools
import math

import jax
import jax.numpy as jnp
from jax import lax
from jax.experimental import pallas as pl
from jax.experimental.pallas import tpu as pltpu
from jax.sharding import PartitionSpec as P

CBLOCK = 512
SBLOCK = 256
REACH = 2
BANDS = 16
COL_SIDE = 32
DEPTH_RANGE = 2.0
DEPTH_SHIFT = 0.25
DAMPING = 1.0
GUARD = 1e-06

SPAN = 2 * REACH + 1
CHUNKS = 4
HOPS = tuple(r for r in range(-REACH, REACH + 1) if r != 0)
UNROLL = 8
KEPT = 88
LAG = 2
STRIP = 64
STRETCH = 4.0
MESH = pl.DeviceIdType.MESH
F32 = jnp.float32
BF16 = jnp.bfloat16
VMEM_LIMIT = 4 * 1024 * 1024


def in_groups(size, body, start):
    group = math.gcd(size, 4)

    def several(k, carry):
        for m in range(group):
            carry = body(k * group + m, carry)
        return carry
    return lax.fori_loop(0, size // group, several, start)


def exists(me, r, n):
    return jnp.logical_and(me + r >= 0, me + r < n)


def split(x):
    high = x.astype(BF16)
    return high, (x - high.astype(F32)).astype(BF16)


def lane_sums(x):
    total = jnp.sum(x, axis=0, keepdims=True)
    out = total[:, 0:128]
    for k in range(1, x.shape[1] // 128):
        out = out + total[:, k * 128 : (k + 1) * 128]
    return out


def exchange_kernel(
    n, scale, blocks, dirn_hbm, pairs, band_hbm, offs_hbm,
    st_o, entries_o, v_o, f_o, z_o, norm_o, codes_o,
    dirn, band, offs, in_sem, send_sem, recv_sem,
):
    me = lax.axis_index("tile")
    rows = pairs.shape[0]
    part = dirn.shape[1] // CHUNKS
    fetch_offs = pltpu.make_async_copy(offs_hbm, offs, in_sem.at[0])
    fetch_pairs = pltpu.make_async_copy(pairs, codes_o.at[REACH], in_sem.at[1])
    fetch_band = pltpu.make_async_copy(band_hbm, band, in_sem.at[2])
    fetch_dirn = [
        pltpu.make_async_copy(
            dirn_hbm.at[:, k * part : (k + 1) * part],
            dirn.at[:, k * part : (k + 1) * part],
            in_sem.at[3 + k],
        )
        for k in range(CHUNKS)
    ]
    for one in [fetch_offs, fetch_pairs, fetch_band] + fetch_dirn:
        one.start()
    barrier = pltpu.get_barrier_semaphore()
    for r in HOPS:
        @pl.when(exists(me, r, n))
        def _():
            pl.semaphore_signal(barrier, inc=1, device_id={"tile": me + r}, device_id_type=MESH)

    own = REACH * rows
    for r in HOPS:
        @pl.when(jnp.logical_not(exists(me, r, n)))
        def _():
            t = r + REACH
            st_o[:, t * rows : (t + 1) * rows] = jnp.zeros((2, rows, SBLOCK), F32)
            codes_o[t] = jnp.full(codes_o.shape[1:], -1, jnp.int32)
    fetch_offs.wait()
    for k in range(rows):
        for w in range(2):
            st_o[w, own + k : own + k + 1] = offs[w : w + 1, k * SBLOCK : (k + 1) * SBLOCK]
    fetch_pairs.wait()

    peers = sum(exists(me, r, n).astype(jnp.int32) for r in HOPS)
    pl.semaphore_wait(barrier, peers)

    def copies(q, r):
        t = REACH - r
        made = []
        for which, (src, dst) in enumerate((
            (codes_o.at[REACH], codes_o.at[t]),
            (st_o.at[:, pl.ds(own, rows)], st_o.at[:, pl.ds(t * rows, rows)]),
        )):
            made.append(pltpu.make_async_remote_copy(
                src_ref=src, dst_ref=dst, send_sem=send_sem.at[which, q],
                recv_sem=recv_sem.at[which, q], device_id={"tile": me + r}, device_id_type=MESH,
            ))
        return made

    for q, r in enumerate(HOPS):
        @pl.when(exists(me, r, n))
        def _():
            for one in copies(q, r):
                one.start()

    fetch_band.wait()
    depth = (band[...].astype(F32) + 0.5) * (DEPTH_RANGE / BANDS)
    shifted = depth + DEPTH_SHIFT
    f_o[...] = (scale * STRETCH**3) * depth * (shifted * jnp.sqrt(shifted))
    q = lax.bitwise_and(lax.broadcasted_iota(jnp.int32, z_o.shape, 0), 3).astype(F32)
    z_o[...] = (STRETCH * STRETCH) * (depth * depth) + 0.25 * (q * q)

    def block(first, b, total):
        b = first + b
        for q in range(CBLOCK // 128):
            lanes = pl.ds(pl.multiple_of(b * CBLOCK + q * 128, 128), 128)
            values = dirn[:, lanes]
            high, low = split(f_o[pl.ds(b * (CBLOCK // 128) + q, 1), :] * values)
            v_o[b, 0:16, q * 128 : (q + 1) * 128] = high
            v_o[b, 16:32, q * 128 : (q + 1) * 128] = low
            total = total + values * values
        return total

    total = jnp.zeros((dirn.shape[0], 128), F32)
    for k in range(CHUNKS):
        fetch_dirn[k].wait()
        total = in_groups(blocks // CHUNKS, functools.partial(block, k * blocks // CHUNKS), total)
    norm_o[...] = jnp.broadcast_to(lane_sums(total), norm_o.shape)

    for q, r in enumerate(HOPS):
        @pl.when(exists(me, r, n))
        def _():
            for one in copies(q, r):
                one.wait_send()

        @pl.when(exists(me, -r, n))
        def _():
            for one in copies(q, r):
                one.wait_recv()

    codes = codes_o[...]
    slot = lax.broadcasted_iota(jnp.int32, codes.shape, 0)
    hit = lax.shift_right_arithmetic(codes, 5) == SPAN - 1 - slot
    slot = slot * rows + lax.broadcasted_iota(jnp.int32, codes.shape, 1)
    entries_o[...] = jnp.where(hit, slot * 32 + lax.bitwise_and(codes, 31), -1)


def fill_block(entry, slots, places, z, dst):
    j = lax.shift_right_logical(entry, 5)
    b = lax.bitwise_and(entry, 31)
    at = jnp.minimum(j, slots - 1)
    parity = lax.bitwise_and(b, 1).astype(F32)
    lane = lax.broadcasted_iota(jnp.int32, (8, 128), 1)
    unit = STRETCH / COL_SIDE
    cell_across = (lax.rem(lane, COL_SIDE).astype(F32) + 0.5) * unit
    cell_along = (lax.div(lane, COL_SIDE).astype(F32) + 0.5) * unit + (0.5 * STRETCH) * parity
    cell_across = jnp.concatenate([cell_across] * (STRIP // 8), axis=0)
    cell_along = jnp.concatenate([cell_along] * (STRIP // 8), axis=0)
    which = jnp.full((STRIP, 128), at, jnp.int32)
    deeps = [
        jnp.broadcast_to(z[pl.ds(b * (CBLOCK // 128) + q, 1), :], (8, 128))
        for q in range(CBLOCK // 128)
    ]
    for k in range(SBLOCK // STRIP):
        rows = slice(k * STRIP, (k + 1) * STRIP)
        across = jnp.take_along_axis(places[0, rows, :], which, axis=1) - cell_across
        along = jnp.take_along_axis(places[1, rows, :], which, axis=1) - cell_along
        flat = across * across + along * along
        for q in range(CBLOCK // 128):
            if q > 0:
                flat = flat - along
            inverse = lax.rsqrt(flat + jnp.concatenate([deeps[q]] * (STRIP // 8), axis=0))
            high, low = split(inverse * inverse * inverse)
            dst[0, q, rows, :] = high
            dst[1, q, rows, :] = low
    return j, b


def block_part(block, w):
    return jnp.concatenate([block[w, q] for q in range(CBLOCK // 128)], axis=1)


def forward_kernel(entries_in, st, z, v, img, list_out, places, *rest):
    kept = rest[:UNROLL]
    spare, entries, pair_list, in_sem, out_sem = rest[UNROLL:]
    fetch = pltpu.make_async_copy(entries_in, entries, in_sem)
    fetch.start()
    slots = st.shape[1]
    pad = jnp.zeros((128 - slots, SBLOCK), F32)
    shift = lax.broadcasted_iota(jnp.int32, (slots, SBLOCK), 0) // entries.shape[1] - REACH
    places[0] = jnp.concatenate([STRETCH * (st[0] + shift.astype(F32)), pad], axis=0).T
    places[1] = jnp.concatenate([STRETCH * st[1], pad], axis=0).T
    rows = entries.shape[1]
    img[...] = jnp.zeros(img.shape, F32)
    for u in range(UNROLL - LAG, UNROLL):
        kept[u][0] = jnp.zeros(kept[u].shape[1:], BF16)
    fetch.wait()
    nothing = SPAN * rows * 32
    for u in range(UNROLL - LAG, UNROLL):
        pair_list[u] = nothing
    filled = jnp.int32(UNROLL)
    for t in range(SPAN):
        def pick(row, filled):
            for p in range(entries.shape[2]):
                entry = entries[t, row, p]
                pair_list[filled] = entry
                filled = filled + (entry >= 0).astype(jnp.int32)
            return filled
        filled = lax.fori_loop(0, rows, pick, filled)
    for u in range(UNROLL):
        pair_list[filled + u] = nothing
    steps = (filled - 1) // UNROLL
    held = jnp.minimum(steps, KEPT // UNROLL)
    pair_list[0] = steps
    pair_list[1] = held
    leave = pltpu.make_async_copy(pair_list, list_out, out_sem)
    leave.start()

    def multiply(entry, block):
        j = lax.shift_right_logical(entry, 5)
        b = lax.bitwise_and(entry, 31)
        out = jnp.zeros((32, SBLOCK), F32)
        for w in range(2):
            out = out + lax.dot_general(
                v[b], block_part(block, w), (((1,), (1,)), ((), ())), preferred_element_type=F32
            )
        img[j] += out[0:16] + out[16:32]

    def step(i, carry):
        at = (i + 1) * UNROLL
        for u in range(UNROLL):
            fill_block(pair_list[at + u], slots, places, z, kept[u].at[i])
            if u < LAG:
                earlier = kept[UNROLL + u - LAG].at[jnp.maximum(i - 1, 0)]
            else:
                earlier = kept[u - LAG].at[i]
            multiply(pair_list[at + u - LAG], earlier)
        return carry

    def step_over(i, carry):
        for u in range(UNROLL):
            entry = pair_list[(i + 1) * UNROLL + u]
            fill_block(entry, slots, places, z, spare)
            multiply(entry, spare)
        return carry

    lax.fori_loop(0, held, step, 0)
    for u in range(UNROLL - LAG, UNROLL):
        multiply(pair_list[held * UNROLL + u], kept[u].at[jnp.maximum(held - 1, 0)])
    lax.fori_loop(held, steps, step_over, 0)
    leave.wait()


def all_sum(n, me, mine, landing, send_sem, recv_sem, start, finish):
    def made(k):
        return pltpu.make_async_remote_copy(
            src_ref=mine, dst_ref=landing.at[k], send_sem=send_sem.at[k], recv_sem=recv_sem.at[k],
            device_id={"tile": lax.rem(me + k, n)}, device_id_type=MESH,
        )
    if start:
        def go(k, c):
            made(k).start()
            return c
        lax.fori_loop(1, n, go, 0)
    if finish:
        def done(k, c):
            made(k).wait()
            return c
        lax.fori_loop(1, n, done, 0)


def greet(n, me):
    barrier = pltpu.get_barrier_semaphore()

    def one(k, c):
        pl.semaphore_signal(
            barrier, inc=1, device_id={"tile": lax.rem(me + k, n)}, device_id_type=MESH
        )
        return c
    lax.fori_loop(1, n, one, 0)


def greeted(n):
    pl.semaphore_wait(pltpu.get_barrier_semaphore(), n - 1)


def image_kernel(
    n, rows, img, res_hbm, norm, old_hbm, newres_o, scal_o,
    res, old, in_sem, transit, joined, part_rx, norm_tx, norm_rx, send_sem, recv_sem, nsend_sem, nrecv_sem,
):
    me = lax.axis_index("tile")
    greet(n, me)
    fetch_old = pltpu.make_async_copy(old_hbm, old, in_sem.at[0])
    fetch_res = pltpu.make_async_copy(res_hbm, res, in_sem.at[1])
    fetch_old.start()
    fetch_res.start()
    greeted(n)
    s = 1 - 2 * lax.rem(me, 2)
    outward = exists(me, -2 * s, n)
    inward = exists(me, 2 * s, n)

    def slab(ref, r):
        return ref.at[pl.ds((REACH + r) * rows, rows)]

    def copy(number, src, dst, to):
        return pltpu.make_async_remote_copy(
            src_ref=src, dst_ref=dst, send_sem=send_sem.at[number],
            recv_sem=recv_sem.at[number], device_id={"tile": to}, device_id_type=MESH,
        )

    to_join = copy(0, slab(img, 2 * s), transit, me + s)
    to_sibling = copy(1, slab(img, s), part_rx.at[0], me + s)
    to_far = copy(2, slab(img, -2 * s), part_rx.at[1], me - 2 * s)
    to_near = copy(3, joined, part_rx.at[2], me - s)
    own = slab(newres_o, 0)
    give_near = copy(4, own, slab(newres_o, s), me - s)
    give_far = copy(5, own, slab(newres_o, -2 * s), me + 2 * s)
    give_sibling = copy(6, own, slab(newres_o, -s), me + s)
    pass_on = copy(7, slab(newres_o, -s), slab(newres_o, -2 * s), me + s)

    @pl.when(inward)
    def _():
        to_join.start()

    @pl.when(outward)
    def _():
        to_far.start()
    to_sibling.start()

    def squares(k, total):
        values = old[:, pl.ds(pl.multiple_of(k * 512, 512), 512)]
        return total + values * values

    fetch_old.wait()
    fetch_res.wait()
    before = in_groups(old.shape[1] // 512, squares, jnp.zeros((old.shape[0], 512), F32))
    lane = lax.broadcasted_iota(jnp.int32, (1, 128), 1)
    gamma_part = jnp.sum(lane_sums(before), axis=1, keepdims=True)
    norm_part = DAMPING * jnp.sum(norm[0:1, :], axis=1, keepdims=True)
    known = jnp.where(lane == 0, gamma_part, jnp.where(lane == 1, norm_part, 0.0))

    @pl.when(outward)
    def _():
        to_join.wait_recv()
        joined[...] = transit[...] + img[pl.ds((REACH - s) * rows, rows)]
        to_near.start()

    to_sibling.wait_recv()
    here = REACH * rows
    newres_o[here : here + rows] = img[here : here + rows] + part_rx[0]

    @pl.when(inward)
    def _():
        to_far.wait_recv()
        newres_o[here : here + rows] += part_rx[1]

    @pl.when(outward)
    def _():
        to_near.wait_recv()
        newres_o[here : here + rows] += part_rx[2]

    image = newres_o[here : here + rows]
    squared = lane_sums(jnp.sum(image * image, axis=0))
    folded = squared + jnp.where(lane == 1, 0.0, pltpu.roll(jnp.where(lane < 2, squared, 0.0), 2, 1))
    norm_tx[...] = jnp.where(lane < 2, known, folded)
    all_sum(n, me, norm_tx, norm_rx, nsend_sem, nrecv_sem, True, True)
    norm_rx[0] = norm_tx[...]
    totals = jnp.sum(norm_rx[...], axis=0)
    gamma_old = jnp.sum(jnp.where(lane == 0, totals, 0.0), axis=1, keepdims=True)
    curvature = jnp.sum(jnp.where(lane == 0, 0.0, totals), axis=1, keepdims=True)
    length = gamma_old / (curvature + GUARD)
    scal_o[...] = jnp.concatenate(
        [jnp.broadcast_to(length, (4, 128)), jnp.broadcast_to(gamma_old, (4, 128))], axis=0
    )
    for k in range(rows):
        newres_o[here + k] = res[:, k * SBLOCK : (k + 1) * SBLOCK] - length * newres_o[here + k]

    @pl.when(outward)
    def _():
        give_near.start()

    @pl.when(inward)
    def _():
        give_far.start()
    give_sibling.start()

    @pl.when(outward)
    def _():
        give_near.wait_recv()
        pass_on.start()
        to_far.wait_send()
        to_near.wait_send()
        give_far.wait_recv()
        give_near.wait_send()
        pass_on.wait_send()

    @pl.when(inward)
    def _():
        to_join.wait_send()
        give_far.wait_send()
        pass_on.wait_recv()
    to_sibling.wait_send()
    give_sibling.wait()


def adjoint_kernel(list_in, places, z, newres, scal, model_in, dirn_in, *rest):
    kept = rest[:UNROLL]
    model_hbm, model_o, acc, res_hbm, pair_list, res_o, dirn, parts, spare, in_sem, out_sem = rest[UNROLL:]
    slots = newres.shape[0]
    rows = slots // SPAN
    fetch_model = pltpu.make_async_copy(model_in, model_o, in_sem.at[0])
    fetch_dirn = pltpu.make_async_copy(dirn_in, dirn, in_sem.at[1])
    fetch_list = pltpu.make_async_copy(list_in, pair_list, in_sem.at[2])
    fetch_list.start()
    fetch_model.start()
    fetch_dirn.start()
    for k in range(rows):
        res_o[:, k * SBLOCK : (k + 1) * SBLOCK] = newres[REACH * rows + k]
    leave_res = pltpu.make_async_copy(res_o, res_hbm, out_sem.at[1])
    leave_res.start()

    def cut(k, c):
        high, low = split(newres[k])
        parts[k, 0:16, :] = high
        parts[k, 16:32, :] = low
        return c
    in_groups(slots, cut, 0)
    parts[slots] = jnp.zeros((32, SBLOCK), BF16)
    acc[...] = jnp.zeros(acc.shape, F32)

    def add_pair(j, b, block):
        out = jnp.zeros((32, CBLOCK), F32)
        for w in range(2):
            out = out + jnp.dot(parts[j], block_part(block, w), preferred_element_type=F32)
        acc[b] += out[0:16] + out[16:32]

    def reread(i, carry):
        for u in range(UNROLL):
            entry = pair_list[(i + 1) * UNROLL + u]
            add_pair(lax.shift_right_logical(entry, 5), lax.bitwise_and(entry, 31), kept[u].at[i])
        return carry

    def rebuild(i, carry):
        for u in range(UNROLL):
            j, b = fill_block(pair_list[(i + 1) * UNROLL + u], slots, places, z, spare)
            add_pair(j, b, spare)
        return carry

    fetch_list.wait()
    steps = pair_list[0]
    held = pair_list[1]
    first = jnp.minimum(held, 1)
    lax.fori_loop(0, first, reread, 0)
    fetch_model.wait()
    fetch_dirn.wait()
    length = scal[0:1, 0:1]

    def update(b, c):
        lanes = pl.ds(pl.multiple_of(b * CBLOCK, CBLOCK), CBLOCK)
        model_o[:, lanes] = model_o[:, lanes] + length * dirn[:, lanes]
        return c
    in_groups(acc.shape[0], update, 0)
    leave = pltpu.make_async_copy(model_o, model_hbm, out_sem.at[0])
    leave.start()
    twice = (held - first) // 2

    def reread_two(k, carry):
        return reread(first + 2 * k + 1, reread(first + 2 * k, carry))

    lax.fori_loop(0, twice, reread_two, 0)
    lax.fori_loop(first + 2 * twice, held, reread, 0)
    lax.fori_loop(held, steps, rebuild, 0)
    leave_res.wait()
    leave.wait()


def gamma_kernel(n, acc, model, f, scal, grad_o, ratio_o, mine, landing, send_sem, recv_sem):
    me = lax.axis_index("tile")
    greet(n, me)

    def finish(b, total):
        lanes = pl.ds(pl.multiple_of(b * CBLOCK, CBLOCK), CBLOCK)
        factor = jnp.concatenate(
            [f[pl.ds(b * (CBLOCK // 128) + q, 1), :] for q in range(CBLOCK // 128)], axis=1
        )
        gradient = factor * acc[b] - DAMPING * model[:, lanes]
        grad_o[:, lanes] = gradient
        return total + gradient * gradient

    total = in_groups(acc.shape[0], finish, jnp.zeros((model.shape[0], CBLOCK), F32))
    mine[...] = lane_sums(total)
    greeted(n)
    all_sum(n, me, mine, landing, send_sem, recv_sem, True, True)
    landing[0] = mine[...]
    total = jnp.sum(jnp.sum(landing[...], axis=0), axis=1, keepdims=True)
    ratio_o[...] = total / (scal[4:5, 0:1] + GUARD)


def shards(model_field, direction, old_grad, residual, block_pairs, depth_band, station_offsets):
    n = lax.axis_size("tile")
    epochs, cells = model_field.shape
    stations = residual.shape[1]
    rows = block_pairs.shape[0]
    pairs = block_pairs.shape[1]
    blocks = cells // CBLOCK
    scale = 2.0 / math.sqrt(cells)
    vmem = pl.BlockSpec(memory_space=pltpu.VMEM)
    smem = pl.BlockSpec(memory_space=pltpu.SMEM)
    hbm = pl.BlockSpec(memory_space=pltpu.HBM)
    shape = jax.ShapeDtypeStruct
    slots = SPAN * rows
    listed = slots * pairs + 2 * UNROLL
    one_block = (2, CBLOCK // 128, SBLOCK, 128)
    dma = pltpu.SemaphoreType.DMA

    def in_hbm(one):
        return pltpu.with_memory_space_constraint(one, pltpu.HBM)

    def params(number=None):
        if number is None:
            return pltpu.CompilerParams(vmem_limit_bytes=VMEM_LIMIT)
        return pltpu.CompilerParams(
            vmem_limit_bytes=VMEM_LIMIT, collective_id=number, has_side_effects=True
        )

    st, entries, v, f, z, norm = pl.pallas_call(
        functools.partial(exchange_kernel, n, scale, blocks),
        out_shape=(
            shape((2, slots, SBLOCK), F32),
            shape((SPAN, rows, pairs), jnp.int32),
            shape((blocks, 2 * epochs, CBLOCK), BF16),
            shape((cells // 128, 128), F32),
            shape((cells // 128, 128), F32),
            shape((8, 128), F32),
        ),
        in_specs=[hbm] * 4,
        out_specs=(vmem,) * 6,
        scratch_shapes=[
            pltpu.VMEM((SPAN, rows, pairs), jnp.int32),
            pltpu.VMEM((epochs, cells), F32),
            pltpu.VMEM((cells // 128, 128), jnp.int32),
            pltpu.VMEM((2, stations), F32),
            dma((3 + CHUNKS,)),
            dma((2, len(HOPS))),
            dma((2, len(HOPS))),
        ],
        compiler_params=params(0),
        name="exchange",
    )(
        in_hbm(direction), in_hbm(block_pairs),
        in_hbm(depth_band.reshape(cells // 128, 128)), in_hbm(station_offsets),
    )

    img, pair_list, places, *kept = pl.pallas_call(
        forward_kernel,
        out_shape=(
            shape((slots + 1, epochs, SBLOCK), F32),
            shape((listed,), jnp.int32),
            shape((2, SBLOCK, 128), F32),
        ) + (pltpu.VMEM((KEPT // UNROLL,) + one_block, BF16),) * UNROLL,
        in_specs=[vmem] * 4,
        out_specs=(vmem, hbm) + (vmem,) * (1 + UNROLL),
        scratch_shapes=[
            pltpu.VMEM(one_block, BF16),
            pltpu.SMEM((SPAN, rows, pairs), jnp.int32),
            pltpu.SMEM((listed,), jnp.int32),
            dma(()),
            dma(()),
        ],
        compiler_params=params(),
        name="forward",
    )(entries, st, z, v)

    kept = [pltpu.with_memory_space_constraint(one, pltpu.VMEM) for one in kept]
    newres, scal = pl.pallas_call(
        functools.partial(image_kernel, n, rows),
        out_shape=(shape((slots, epochs, SBLOCK), F32), shape((8, 128), F32)),
        in_specs=[vmem, hbm, vmem, hbm],
        out_specs=(vmem,) * 2,
        scratch_shapes=[
            pltpu.VMEM((epochs, stations), F32),
            pltpu.VMEM((epochs, cells), F32),
            dma((2,)),
            pltpu.VMEM((rows, epochs, SBLOCK), F32),
            pltpu.VMEM((rows, epochs, SBLOCK), F32),
            pltpu.VMEM((3, rows, epochs, SBLOCK), F32),
            pltpu.VMEM((1, 128), F32),
            pltpu.VMEM((n, 1, 128), F32),
            dma((8,)),
            dma((8,)),
            dma((n,)),
            dma((n,)),
        ],
        compiler_params=params(1),
        name="images",
    )(img, in_hbm(residual), norm, in_hbm(old_grad))

    new_model, model_kept, acc, new_residual = pl.pallas_call(
        adjoint_kernel,
        out_shape=(
            shape((epochs, cells), F32),
            shape((epochs, cells), F32),
            shape((blocks, epochs, CBLOCK), F32),
            shape((epochs, stations), F32),
        ),
        in_specs=[pl.BlockSpec(memory_space=pl.ANY)] + [vmem] * 4 + [hbm] * 2 + [vmem] * UNROLL,
        out_specs=(hbm, vmem, vmem, hbm),
        scratch_shapes=[
            pltpu.SMEM((listed,), jnp.int32),
            pltpu.VMEM((epochs, stations), F32),
            pltpu.VMEM((epochs, cells), F32),
            pltpu.VMEM((slots + 1, 2 * epochs, SBLOCK), BF16),
            pltpu.VMEM(one_block, BF16),
            dma((3,)),
            dma((2,)),
        ],
        compiler_params=params(),
        name="adjoint",
    )(
        pair_list, places, z, newres, scal, in_hbm(model_field), in_hbm(direction), *kept
    )

    gradient, ratio = pl.pallas_call(
        functools.partial(gamma_kernel, n),
        out_shape=(shape((epochs, cells), F32), shape((1, 1), F32)),
        in_specs=[vmem] * 4,
        out_specs=(vmem,) * 2,
        scratch_shapes=[
            pltpu.VMEM((1, 128), F32), pltpu.VMEM((n, 1, 128), F32), dma((n,)), dma((n,)),
        ],
        compiler_params=params(2),
        name="gamma",
    )(acc, model_kept, f, scal)
    new_direction = gradient + ratio.reshape(()) * direction
    return (new_model, new_residual, new_direction)


def solution(mesh):
    both = ("groups", "tile")
    wide = P(None, both)
    return jax.shard_map(
        shards,
        mesh=mesh,
        in_specs=(wide, wide, wide, wide, P(both, None), P(both), wide),
        out_specs=(wide, wide, wide),
        check_vma=False,
    )
```
